128 devices in a mesh: span: 4 (over z_lo, core), xsec: 32 (over y, x, z_hi).
Axes of the slice: x: 4, y: 4, z: 4 (z_hi: 2, z_lo: 2; z = z_hi * 2 + z_lo), core: 2. Of those that a mesh axis runs over, the one named last changes fastest.
Arguments:
- fwd_modes: bfloat16 [3, 32, 8, 9, 9, 512], P(None, 'xsec', None, None, None, 'span'), may hold values from -6 to 6
- adj_modes: bfloat16 [3, 32, 8, 9, 9, 512], P(None, 'xsec', None, None, None, 'span'), may hold values from -6 to 6
- layer_height: float32 [8], replicated, may hold values from 0.5 to 1
- column_width: float32 [32], P('xsec'), may hold values from 0.5 to 1
- wall_mask: int32 [32, 9], P('xsec'), may hold values 0 or 1
Outputs:
- adj_new: bfloat16 [3, 32, 8, 9, 9, 512], P(None, 'xsec', None, None, None, 'span')
- wall_sens: float32 [32, 9, 512], P('xsec', None, 'span')
The draws below stay inside these ranges and needn't reach their ends.
All inputs are finite; a program needn't handle non-finite values. No bound on the sum of `wall_mask` on one device may be relied on, other than what follows from the above.
Results may differ from the reference program's by a relative error of at most 0.0038.
Values may be sent and summed in bfloat16 or wider, within the bound.
No kernel may reach another device: no remote copies, remote signals or barrier semaphores. Data moves between devices by JAX's collectives and lax.ppermute only.
A program may use at most 192 MiB of HBM per device.

```python
import math
import jax
import jax.numpy as jnp
import numpy as np
from jax import lax

NODES = 9
NK = 512
NR = 8
SUB = 2
NA = 32


def plant(values, stream_key, smallest, largest):
    place = [jax.random.randint(jax.random.fold_in(stream_key, axis), (), 0, length) for axis, length in enumerate(values.shape)]
    longest = values.shape.index(max(values.shape))
    neighbour = place[:longest] + [(place[longest] + 1) % values.shape[longest]] + place[longest + 1:]
    return values.at[tuple(place)].set(smallest).at[tuple(neighbour)].set(largest)


def levels(stream_key, shape, pieces, least, largest):
    gain = 1.0
    for dim, blocks in pieces:
        steps = jax.random.uniform(jax.random.fold_in(jax.random.fold_in(stream_key, 6), dim), (blocks,), jnp.float32, least / len(pieces), largest / len(pieces))
        gain = gain * jnp.repeat(jnp.exp(steps), shape[dim] // blocks).reshape((-1,) + (1,) * (len(shape) - 1 - dim))
    return gain


def gaussian(own_key, shape, deviation, reach, shards=(), held_as=jnp.bfloat16):
    loudness = levels(own_key, shape, shards, -0.22, 0.18) if shards else 1.0
    drawn = jax.random.normal(own_key, shape, jnp.float32) * deviation * loudness
    return jnp.minimum(jnp.maximum(drawn, -reach), reach).astype(held_as)


def setup_inputs(seed: int = 0) -> dict:
    key_list = jax.random.split(jax.random.key(seed), 6)
    fwd_modes = gaussian(key_list[0], (3, NA, NR, NODES, NODES, NK), 1.0, 6.0, ((1, 32), (5, 4)))
    adj_modes = gaussian(key_list[1], (3, NA, NR, NODES, NODES, NK), 1.0, 6.0, ((1, 32), (5, 4)))
    layer_height = jnp.clip(jnp.exp(jax.random.uniform(key_list[2], (NR,), jnp.float32, math.log(0.5), math.log(1.0))), 0.5, 1.0)
    column_width = jnp.clip(jnp.exp(math.log(1.0) - 0.6931472 * jax.random.uniform(key_list[3], (NA,), jnp.float32) ** levels(key_list[3], (NA,), ((0, 32),), -0.2, 0.2)), 0.5, 1.0)
    wall_mask = plant((jax.random.randint(key_list[4], (NA, NODES), 0, 3) < 1).astype(jnp.int32), jax.random.fold_in(key_list[4], 1), 0, 1)
    return dict(fwd_modes=fwd_modes, adj_modes=adj_modes, layer_height=layer_height, column_width=column_width, wall_mask=wall_mask)


ADV_STEP = 0.0025
DIFFUSE = 5e-05
WALL_GAIN = 0.01
SPAN_GAIN = 1.0 / 32.0
HIGHEST = lax.Precision.HIGHEST

def cheb_table(number):
    degree = number - 1
    points = -np.cos(np.pi * np.arange(number) / degree)
    factor = np.where((np.arange(number) == 0) | (np.arange(number) == degree), 2.0, 1.0)
    parity = (-1.0) ** np.arange(number)
    spacing = points[:, None] - points[None, :] + np.eye(number)
    matrix = factor[:, None] * parity[:, None] * parity[None, :] / (factor[None, :] * spacing)
    matrix = matrix * (1.0 - np.eye(number))
    matrix = matrix - np.eye(number) * np.sum(matrix, axis=1)[:, None]
    return matrix.astype(np.float32)

def span_tables(modes):
    indices = np.arange(modes)
    pair_index = indices // 2
    wavenum = np.where(indices == 1, modes // 2, pair_index)
    planes = np.arange(modes)
    phases = 2.0 * np.pi * (wavenum[:, None] * planes[None, :] % modes) / modes
    basis_rows = np.where((indices % 2 == 0)[:, None], np.cos(phases), np.sin(phases))
    basis_rows = np.where((indices <= 1)[:, None], np.cos(phases), basis_rows)
    norm_gain = 1.0 / np.sqrt(modes / 2.0)
    weights_k = np.where(indices <= 1, 1.0, 2.0)
    synthesis = basis_rows * norm_gain
    analysis = (basis_rows * (weights_k / (modes * norm_gain))[:, None]).T
    slopes = np.where(indices <= 1, 0.0, pair_index * SPAN_GAIN)
    kappa_sq = (wavenum * SPAN_GAIN) ** 2
    return (synthesis.astype(np.float32), analysis.astype(np.float32), slopes.astype(np.float32), kappa_sq.astype(np.float32))

def span_slope(values, slopes):
    full_shape = values.shape
    paired = values.astype(jnp.float32).reshape(full_shape[:-1] + (full_shape[-1] // 2, 2))
    pair_rates = slopes.reshape(full_shape[-1] // 2, 2)
    turned = jnp.stack([pair_rates[:, 0] * paired[..., 1], -pair_rates[:, 1] * paired[..., 0]], axis=-1)
    return turned.reshape(full_shape)

def radial(field, heights):
    derive = jnp.asarray(cheb_table(NODES))
    slope_rows = jnp.einsum('il,carljk->carijk', derive, field, precision=HIGHEST)
    return slope_rows * (2.0 / heights)[None, None, :, None, None, None]

def azimuthal(field, widths):
    derive = jnp.asarray(cheb_table(NODES))
    slope_rows = jnp.einsum('jl,carilk->carijk', derive, field, precision=HIGHEST)
    return slope_rows * (2.0 / widths)[None, :, None, None, None, None]

def planar_force(fwd, adj, fwd_dz, adj_dz, heights, widths, synth_bf, synth_fl, analysis):
    fwd_planes = jnp.dot(fwd, synth_bf, preferred_element_type=jnp.float32)
    adj_planes = jnp.dot(adj, synth_bf, preferred_element_type=jnp.float32)
    fwd_zplanes = jnp.dot(fwd_dz, synth_fl, precision=HIGHEST)
    adj_zplanes = jnp.dot(adj_dz, synth_fl, precision=HIGHEST)
    fwd_dirs = (radial(fwd_planes, heights), azimuthal(fwd_planes, widths), fwd_zplanes)
    adj_dirs = (radial(adj_planes, heights), azimuthal(adj_planes, widths), adj_zplanes)
    carried = fwd_planes[0] * adj_dirs[0] + fwd_planes[1] * adj_dirs[1] + fwd_planes[2] * adj_dirs[2]
    pulled = jnp.stack([adj_planes[0] * fwd_dirs[direc][0] + adj_planes[1] * fwd_dirs[direc][1] + adj_planes[2] * fwd_dirs[direc][2] for direc in range(3)])
    force = carried - pulled
    return jnp.dot(force, analysis, precision=HIGHEST).astype(jnp.bfloat16)

def radial_average(field):
    shared = (field[:, :, :-1, -1] + field[:, :, 1:, 0]) * 0.5
    field = field.at[:, :, :-1, -1].set(shared)
    return field.at[:, :, 1:, 0].set(shared)

def cyclic_average(field):
    field = radial_average(field)
    left_face = field[:, :, :, :, 0]
    right_face = field[:, :, :, :, -1]
    before = jnp.roll(right_face, 1, axis=1)
    after = jnp.roll(left_face, -1, axis=1)
    field = field.at[:, :, :, :, 0].set((left_face + before) * 0.5)
    return field.at[:, :, :, :, -1].set((right_face + after) * 0.5)

def diffuse(adj_in, force, kappa_sq, heights, widths, grad_average, lap_average):
    adjoint = adj_in.astype(jnp.float32)
    forcing = ADV_STEP * force.astype(jnp.float32)
    for substep in range(SUB):
        grads = jnp.concatenate([radial(adjoint, heights), azimuthal(adjoint, widths)], 0)
        grads = grad_average(grads)
        laplace = radial(grads[:3], heights) + azimuthal(grads[3:], widths) - kappa_sq * adjoint
        laplace = lap_average(laplace)
        adjoint = adjoint + forcing + DIFFUSE * laplace
        adjoint = adjoint.at[:, :, 0, 0].set(0.0)
    return adjoint

def wall_gradient(adjoint, wall_mask, heights):
    derive = jnp.asarray(cheb_table(NODES))
    wall_rows = jnp.einsum('l,albk->abk', derive[0], adjoint[0, :, 0], precision=HIGHEST)
    return WALL_GAIN * (2.0 / heights[0]) * wall_mask.astype(jnp.float32)[:, :, None] * wall_rows

def reference(fwd_modes, adj_modes, layer_height, column_width, wall_mask):
    synthesis, analysis, slopes, kappa_sq = span_tables(NK)
    synth_bf = jnp.asarray(synthesis).astype(jnp.bfloat16)
    synth_fl = jnp.asarray(synthesis)
    analysis_fl = jnp.asarray(analysis)
    slope_all = jnp.asarray(slopes)

    def per_column(items):
        fwd_col, adj_col, width_col = items
        fwd_col = fwd_col[:, None]
        adj_col = adj_col[:, None]
        result = planar_force(fwd_col, adj_col, span_slope(fwd_col, slope_all), span_slope(adj_col, slope_all), layer_height, width_col[None], synth_bf, synth_fl, analysis_fl)
        return result[:, 0]
    force = lax.map(per_column, (jnp.moveaxis(fwd_modes, 1, 0), jnp.moveaxis(adj_modes, 1, 0), column_width))
    force_modes = jnp.moveaxis(force, 0, 1)
    block = min(NK, 16)
    blocks = NK // block

    def split_modes(field):
        return jnp.moveaxis(field.reshape(field.shape[:-1] + (blocks, block)), -2, 0)

    def join_modes(field):
        moved = jnp.moveaxis(field, 0, -2)
        return moved.reshape(moved.shape[:-2] + (NK,))

    def per_block(items):
        adj_block, force_block, kappa_block = items
        adjoint = diffuse(adj_block, force_block, kappa_block, layer_height, column_width, cyclic_average, cyclic_average)
        return (adjoint.astype(jnp.bfloat16), wall_gradient(adjoint, wall_mask, layer_height))
    adj_parts, wall_parts = lax.map(per_block, (split_modes(adj_modes), split_modes(force_modes), split_modes(jnp.asarray(kappa_sq))))
    return (join_modes(adj_parts), join_modes(wall_parts))
```

```python
import functools

import jax
import jax.numpy as jnp
import numpy as np
from jax import lax
from jax.experimental import pallas as pl
from jax.experimental.pallas import tpu as pltpu
from jax.sharding import PartitionSpec as P

NODES = 9
NK = 512
ADV_STEP = 0.0025
DIFFUSE = 5e-05
WALL_GAIN = 0.01
SPAN_GAIN = 1.0 / 32.0
PLANE = NODES * NODES
PAD = 88
ROWS = 3 * 2 * PAD
POINTS = 3 * PLANE * 8
COLS = 3 * NODES
F32 = jnp.float32
BF16 = jnp.bfloat16
MIB = 1 << 20


def cheb_table(number):
    degree = number - 1
    points = -np.cos(np.pi * np.arange(number) / degree)
    factor = np.where((np.arange(number) == 0) | (np.arange(number) == degree), 2.0, 1.0)
    parity = (-1.0) ** np.arange(number)
    spacing = points[:, None] - points[None, :] + np.eye(number)
    matrix = factor[:, None] * parity[:, None] * parity[None, :] / (factor[None, :] * spacing)
    matrix = matrix * (1.0 - np.eye(number))
    matrix = matrix - np.eye(number) * np.sum(matrix, axis=1)[:, None]
    return matrix.astype(np.float32)


def span_tables(modes):
    indices = np.arange(modes)
    pair_index = indices // 2
    wavenum = np.where(indices == 1, modes // 2, pair_index)
    planes = np.arange(modes)
    phases = 2.0 * np.pi * (wavenum[:, None] * planes[None, :] % modes) / modes
    basis_rows = np.where((indices % 2 == 0)[:, None], np.cos(phases), np.sin(phases))
    basis_rows = np.where((indices <= 1)[:, None], np.cos(phases), basis_rows)
    norm_gain = 1.0 / np.sqrt(modes / 2.0)
    weights_k = np.where(indices <= 1, 1.0, 2.0)
    synthesis = (basis_rows * norm_gain).astype(np.float32)
    analysis = ((basis_rows * (weights_k / (modes * norm_gain))[:, None]).T).astype(np.float32)
    slopes = np.where(indices <= 1, 0.0, pair_index * SPAN_GAIN).astype(np.float32)
    kappa_sq = ((wavenum * SPAN_GAIN) ** 2).astype(np.float32)
    return synthesis, analysis, slopes, kappa_sq


def halves(table):
    high = table.astype(jnp.bfloat16)
    return high, (table.astype(np.float64) - high.astype(np.float64)).astype(jnp.bfloat16)


DERIV = cheb_table(NODES).astype(np.float64)
INNER = DERIV[:, 1:8] @ DERIV[1:8, :]
FACED = INNER + 0.5 * np.outer(DERIV[:, 0], DERIV[0]) + 0.5 * np.outer(DERIV[:, 8], DERIV[8])


def plane_tables():
    synthesis, analysis, slopes, kappa_sq = span_tables(NK)
    wave = np.zeros((NK, NK))
    wave[1::2] = slopes[0::2, None].astype(np.float64) * synthesis[0::2]
    wave[0::2] = -slopes[1::2, None].astype(np.float64) * synthesis[1::2]
    radial = np.kron(DERIV, np.eye(NODES))
    around = np.kron(np.eye(NODES), DERIV)
    both = np.zeros((2, 2, PAD, 2, PAD))
    for layer in range(2):
        both[0, layer, :PLANE, layer, :PLANE] = radial
        both[1, layer, :PLANE, layer, :PLANE] = around
    high, low = halves(both.reshape(4 * PAD, 2 * PAD))
    slope = np.concatenate([high, low, high], axis=1)
    kappa = np.broadcast_to(kappa_sq.reshape(4, 1, 128), (4, 8, 128)).astype(np.float32)
    return synthesis.astype(jnp.bfloat16), halves(wave), slope, halves(analysis), kappa


def smem():
    return pl.BlockSpec(memory_space=pltpu.SMEM)


def vmem():
    return pl.BlockSpec(memory_space=pltpu.VMEM)


def call(kernel, name, outs, scratch, specs, flops, nbytes):
    return pl.pallas_call(
        kernel,
        out_shape=[jax.ShapeDtypeStruct(shape, kind) for shape, kind in outs],
        in_specs=specs,
        out_specs=[vmem() for _ in outs],
        scratch_shapes=scratch,
        compiler_params=pltpu.CompilerParams(vmem_limit_bytes=40 * MIB),
        cost_estimate=pl.CostEstimate(flops=flops, bytes_accessed=nbytes, transcendentals=0),
        name=name,
    )


def repack_kernel(pos_ref, x_ref, *refs):
    outs, wide = refs[:4], refs[4]
    pos = pos_ref[0]
    wide[pl.ds(0, POINTS), :] = x_ref[...].astype(F32)
    keep = lax.broadcasted_iota(jnp.int32, (PAD, 128), 0) < PLANE
    for flip, out in enumerate(outs):
        group = pos ^ flip
        for comp in range(3):
            parts = []
            for layer in range(2):
                start = comp * PLANE * 8 + 2 * group + layer
                rows = wide[pl.ds(start, PAD, stride=8), :]
                parts.append(jnp.where(keep, rows, 0.0))
            block = jnp.concatenate(parts, axis=0).astype(BF16)
            out[comp * 2 * PAD : (comp + 1) * 2 * PAD, :] = block


def repack(pos, field, name):
    return call(
        repack_kernel,
        name,
        [((ROWS, 128), BF16)] * 4,
        [pltpu.VMEM((POINTS + 56, 128), F32)],
        [smem(), vmem()],
        1_000_000,
        1_000_000,
    )(pos, field)


def force_kernel(
    pos_ref, height_ref, width_ref, *refs
):
    fwd, adj = refs[0:4], refs[4:8]
    synth_ref, wave_hi_ref, wave_lo_ref, slope_ref, an_hi_ref, an_lo_ref = refs[8:14]
    outs = refs[14:18]
    planes, zplanes, grads, force = refs[18:22]
    pos = pos_ref[0]

    def gather(ref):
        parts = [ref[pl.ds(pl.multiple_of(128 * (pos ^ flip), 128), 128), :] for flip in range(4)]
        return jnp.concatenate(parts, axis=0)

    synth, wave_hi, wave_lo = gather(synth_ref), gather(wave_hi_ref), gather(wave_lo_ref)
    slope = slope_ref[...]
    for which, chunks in ((0, fwd), (1, adj)):
        modes = jnp.concatenate([chunk[...] for chunk in chunks], axis=1)
        planes[which] = jnp.dot(modes, synth, preferred_element_type=F32)
        zplanes[which] = jnp.dot(modes, wave_hi, preferred_element_type=F32) + jnp.dot(
            modes, wave_lo, preferred_element_type=F32
        )
        for comp in range(3):
            block = planes[which, comp * 2 * PAD : (comp + 1) * 2 * PAD, :]
            high = block.astype(BF16)
            low = (block - high.astype(F32)).astype(BF16)
            stack = jnp.concatenate([high, high, low], axis=0)
            grads[which, comp] = jnp.dot(slope, stack, preferred_element_type=F32)

    across = 2.0 / jnp.full((8, 128), width_ref[0], F32)
    for layer in range(2):
        along = 2.0 / jnp.full((8, 128), height_ref[2 * pos + layer], F32)
        for tile in range(PAD // 8):
            row = layer * PAD + 8 * tile
            for lane in range(0, NK, 128):
                lanes = slice(lane, lane + 128)

                def plane(which, comp):
                    at = comp * 2 * PAD + row
                    return planes[which, at : at + 8, lanes]

                def zplane(which, comp):
                    at = comp * 2 * PAD + row
                    return zplanes[which, at : at + 8, lanes]

                def grad(which, direc, comp):
                    at = direc * 2 * PAD + row
                    return grads[which, comp, at : at + 8, lanes]

                fwd_r = plane(0, 0) * along
                fwd_t = plane(0, 1) * across
                fwd_z = plane(0, 2)
                adj_p = [plane(1, comp) for comp in range(3)]
                pulled = [
                    along * sum(adj_p[comp] * grad(0, 0, comp) for comp in range(3)),
                    across * sum(adj_p[comp] * grad(0, 1, comp) for comp in range(3)),
                    sum(adj_p[comp] * zplane(0, comp) for comp in range(3)),
                ]
                for comp in range(3):
                    carried = (
                        fwd_r * grad(1, 0, comp) + fwd_t * grad(1, 1, comp) + fwd_z * zplane(1, comp)
                    )
                    at = comp * 2 * PAD + row
                    force[at : at + 8, lanes] = carried - pulled[comp]

    def pick(ref):
        return jnp.concatenate([ref[pos ^ flip] for flip in range(4)], axis=1)

    an_hi, an_lo = pick(an_hi_ref), pick(an_lo_ref)
    total = force[...]
    high = total.astype(BF16)
    low = (total - high.astype(F32)).astype(BF16)
    result = (
        jnp.dot(high, an_hi, preferred_element_type=F32)
        + jnp.dot(low, an_hi, preferred_element_type=F32)
        + jnp.dot(high, an_lo, preferred_element_type=F32)
    ).astype(BF16)
    for flip, out in enumerate(outs):
        out[...] = result[:, 128 * flip : 128 * (flip + 1)]


def forcing(pos, heights, widths, fwd, adj, tables):
    synth, (wave_hi, wave_lo), slope, (an_hi, an_lo) = tables
    split = lambda table: jnp.asarray(table.reshape(NK, 4, 128).transpose(1, 0, 2))
    constants = [
        jnp.asarray(synth),
        jnp.asarray(wave_hi),
        jnp.asarray(wave_lo),
        jnp.asarray(slope),
        split(an_hi),
        split(an_lo),
    ]
    return call(
        force_kernel,
        "adjoint_forcing",
        [((ROWS, 128), BF16)] * 4,
        [
            pltpu.VMEM((2, ROWS, NK), F32),
            pltpu.VMEM((2, ROWS, NK), F32),
            pltpu.VMEM((2, 3, 4 * PAD, NK), F32),
            pltpu.VMEM((ROWS, NK), F32),
        ],
        [smem(), smem(), smem()] + [vmem()] * 14,
        5_000_000_000,
        8_000_000,
    )(pos, heights, widths, *fwd, *adj, *constants)


def mirror(matrix):
    even = np.concatenate(
        [0.5 * (matrix[:5, :4] + matrix[:5, :4:-1]), matrix[:5, 4:5]], axis=1
    )
    odd = 0.5 * (matrix[:4, :4] - matrix[:4, :4:-1])
    return even, odd


def weighted(coeffs, values):
    total = None
    for coeff, value in zip(coeffs, values):
        term = float(coeff) * value
        total = term if total is None else total + term
    return total


def parity(values):
    even = [values[n] + values[8 - n] for n in range(4)] + [values[4]]
    odd = [values[n] - values[8 - n] for n in range(4)]
    return even, odd


def ends(even, odd):
    row_even = np.concatenate([0.5 * (DERIV[0, :4] + DERIV[0, :4:-1]), DERIV[0, 4:5]])
    row_odd = 0.5 * (DERIV[0, :4] - DERIV[0, :4:-1])
    first, second = weighted(row_even, even), weighted(row_odd, odd)
    return second + first, second - first


def unfold(even, odd):
    low = [even[n] + odd[n] for n in range(4)]
    high = [even[n] - odd[n] for n in range(4)]
    return low + [even[4]] + high[::-1]


def layer_vectors(height_ref):
    layer = lax.broadcasted_iota(jnp.int32, (8, 128), 0)
    height = jnp.full((8, 128), height_ref[0], F32)
    for index in range(1, 8):
        height = jnp.where(layer == index, height_ref[index], height)
    along = 2.0 / height
    below = pltpu.roll(along, 1, 0)
    above = pltpu.roll(along, 7, 0)
    bottom, top = layer == 0, layer == 7
    own_low = jnp.where(bottom, 1.0, 0.5)
    own_high = jnp.where(top, 1.0, 0.5)
    from_below = jnp.where(bottom, 0.0, 0.5)
    from_above = jnp.where(top, 0.0, 0.5)
    return dict(
        layer=layer,
        along=along,
        own_low=own_low,
        own_high=own_high,
        from_below=from_below,
        from_above=from_above,
        grad_below=from_below * below / along,
        grad_above=from_above * above / along,
    )


def local_step(vec, width, kappa, load, store, sent, two_away, visc, faces):
    across = 2.0 / jnp.full((8, 128), width, F32)
    scale_t = DIFFUSE * across * across
    scale_r = DIFFUSE * vec["along"] * vec["along"]
    scale_k = DIFFUSE * kappa
    even_t, odd_t = mirror(FACED)
    even_r, odd_r = mirror(INNER)
    mix_even = 0.5 * (DERIV[:5, 0] - DERIV[:5, 8])
    mix_odd = 0.5 * (DERIV[:4, 0] + DERIV[:4, 8])

    def shared(low, high):
        low_new = vec["own_low"] * low + vec["from_below"] * pltpu.roll(high, 1, 0)
        high_new = vec["own_high"] * high + vec["from_above"] * pltpu.roll(low, 7, 0)
        return low_new, high_new

    right_ref, left_ref = sent
    right_far, left_far = two_away

    for comp in range(3):
        edge_low, edge_high = [], []
        for i in range(NODES):
            values = [load(comp, i, j) for j in range(NODES)]
            even, odd = parity(values)
            low, high = ends(even, odd)
            edge_low.append(across * low)
            edge_high.append(across * high)
            even_out = [weighted(even_t[n], even) for n in range(5)]
            odd_out = [weighted(odd_t[n], odd) for n in range(4)]
            for j, value in enumerate(unfold(even_out, odd_out)):
                visc[pl.ds(8 * (i * NODES + j), 8), :] = scale_t * value
        for edge, ref in ((edge_low, 0), (edge_high, 1)):
            edge[0], edge[8] = shared(edge[0], edge[8])
            for i in range(NODES):
                faces[pl.ds(8 * ((ref * 3 + comp) * NODES + i), 8), :] = edge[i]
        for j in range(NODES):
            values = [load(comp, i, j) for i in range(NODES)]
            even, odd = parity(values)
            low, high = ends(even, odd)
            low_mean = vec["own_low"] * low + vec["grad_below"] * pltpu.roll(high, 1, 0)
            high_mean = vec["own_high"] * high + vec["grad_above"] * pltpu.roll(low, 7, 0)
            differ, total = low_mean - high_mean, low_mean + high_mean
            even_out = [
                weighted(even_r[n], even) + float(mix_even[n]) * differ for n in range(5)
            ]
            odd_out = [weighted(odd_r[n], odd) + float(mix_odd[n]) * total for n in range(4)]
            lap = [
                scale_r * value - scale_k * values[i] + visc[pl.ds(8 * (i * NODES + j), 8), :]
                for i, value in enumerate(unfold(even_out, odd_out))
            ]
            lap[0], lap[8] = shared(lap[0], lap[8])
            if j == 0 or j == 8:
                ref, side = (left_ref, 0) if j == 0 else (right_ref, 1)
                for i in range(NODES):
                    edge = faces[pl.ds(8 * ((side * 3 + comp) * NODES + i), 8), :]
                    pair = jnp.concatenate([edge, lap[i]], axis=0).astype(BF16)
                    ref[pl.ds(16 * (comp * NODES + i), 16), :] = pair
            for i in range(NODES):
                step = 0.5 * lap[i] if j == 0 or j == 8 else lap[i]
                store(comp, i, j, values[i], step)
    for side, ref in ((0, left_far), (1, right_far)):
        for block in range(14):
            first = faces[pl.ds(8 * (side * COLS + 2 * block), 8), :]
            if 2 * block + 1 < COLS:
                second = faces[pl.ds(8 * (side * COLS + 2 * block + 1), 8), :]
            else:
                second = jnp.zeros((8, 128), F32)
            ref[pl.ds(16 * block, 16), :] = jnp.concatenate([first, second], axis=0).astype(BF16)
    return across


def spot(comp, i, j):
    return pl.ds(8 * ((comp * NODES + i) * NODES + j), 8)


def first_kernel(pos_ref, height_ref, width_ref, kappa_ref, x_ref, *refs):
    out, right, left, right_far, left_far, wide, visc, faces = refs
    wide[...] = x_ref[...].astype(F32)

    def load(comp, i, j):
        return wide[spot(comp, i, j), :]

    def store(comp, i, j, value, step):
        out[spot(comp, i, j), :] = value + step

    vec = layer_vectors(height_ref)
    kappa = kappa_ref[pos_ref[0]]
    across = local_step(
        vec, width_ref[0], kappa, load, store, (right, left), (right_far, left_far), visc, faces
    )
    high = across.astype(BF16).astype(F32)
    mid = (across - high).astype(BF16).astype(F32)
    low = across - high - mid
    layer = vec["layer"]
    note = jnp.where(layer == 0, high, jnp.where(layer == 1, mid, jnp.where(layer == 2, low, 0.0)))
    block = jnp.concatenate([note, jnp.zeros((8, 128), F32)], axis=0).astype(BF16)
    for ref in (right, left):
        ref[pl.ds(16 * COLS, 16), :] = block


def second_kernel(pos_ref, height_ref, width_ref, kappa_ref, base_ref, *refs):
    chunks = refs[:4]
    out, right, left, right_far, left_far, push, wide, visc, faces = refs[4:]
    pos = pos_ref[0]
    for flip, chunk in enumerate(chunks):
        group = pos ^ flip
        for comp in range(3):
            block = ADV_STEP * chunk[comp * 2 * PAD : (comp + 1) * 2 * PAD, :].astype(F32)
            for layer in range(2):
                start = comp * PLANE * 8 + 2 * group + layer
                push[pl.ds(start, PLANE, stride=8), :] = block[layer * PAD : layer * PAD + PLANE]
    vec = layer_vectors(height_ref)
    off_wall = jnp.where(vec["layer"] == 0, 0.0, 1.0)
    for comp in range(3):
        for i in range(NODES):
            for j in range(NODES):
                at = spot(comp, i, j)
                value = base_ref[at, :] + push[at, :]
                wide[at, :] = value * off_wall if i == 0 else value

    def load(comp, i, j):
        return wide[spot(comp, i, j), :]

    def store(comp, i, j, value, step):
        at = spot(comp, i, j)
        out[at, :] = value + push[at, :] + step

    local_step(
        vec,
        width_ref[0],
        kappa_ref[pos],
        load,
        store,
        (right, left),
        (right_far, left_far),
        visc,
        faces,
    )


def join_step(width, near, far, own, sides, state, store):
    from_left, from_right = near
    far_left, far_right = far
    own_right, own_left = own
    across = 2.0 / jnp.full((8, 128), width, F32)
    gain = (0.5 * DIFFUSE) * across
    gain_left, gain_right = (0.5 * DIFFUSE) * sides[0], (0.5 * DIFFUSE) * sides[1]
    for block in range(14):
        far_l = far_left[pl.ds(16 * block, 16), :].astype(F32)
        far_r = far_right[pl.ds(16 * block, 16), :].astype(F32)
        for half in range(2):
            col = 2 * block + half
            if col >= COLS:
                continue
            comp, i = divmod(col, NODES)
            at = pl.ds(16 * col, 16)
            pair_l, pair_r = from_left[at, :].astype(F32), from_right[at, :].astype(F32)
            mine_low = own_left[at, :].astype(F32)[0:8]
            mine_high = own_right[at, :].astype(F32)[0:8]
            grad_l, grad_r = gain * pair_l[0:8], gain * pair_r[0:8]
            two_l, two_r = far_l[8 * half : 8 * half + 8], far_r[8 * half : 8 * half + 8]
            for j in range(NODES):
                add = float(DERIV[j, 0]) * grad_l + float(DERIV[j, 8]) * grad_r
                if j == 0:
                    other = gain_left * (float(DERIV[8, 0]) * two_l + float(DERIV[8, 8]) * mine_low)
                    add = 0.5 * (add + pair_l[8:16] + other)
                if j == 8:
                    other = gain_right * (float(DERIV[0, 0]) * mine_high + float(DERIV[0, 8]) * two_r)
                    add = 0.5 * (add + pair_r[8:16] + other)
                store(comp, i, j, state[spot(comp, i, j), :] + add)


def first_join_kernel(width_ref, *refs):
    near, far, own = refs[0:2], refs[2:4], refs[4:6]
    state, out, sides_out = refs[6:9]
    sides = []
    for side, ref in enumerate(near):
        note = ref[pl.ds(16 * COLS, 16), :].astype(F32)[0:8]
        value = jnp.broadcast_to(jnp.sum(note, axis=0, keepdims=True), (8, 128))
        sides_out[pl.ds(8 * side, 8), :] = value
        sides.append(value)

    def store(comp, i, j, value):
        out[spot(comp, i, j), :] = value

    join_step(width_ref[0], near, far, own, sides, state, store)


def second_join_kernel(width_ref, height_ref, mask_ref, *refs):
    near, far, own = refs[0:2], refs[2:4], refs[4:6]
    sides_ref, state, out, wall, full = refs[6:11]
    sides = [sides_ref[pl.ds(0, 8), :], sides_ref[pl.ds(8, 8), :]]
    layer = lax.broadcasted_iota(jnp.int32, (8, 128), 0)
    off_wall = jnp.where(layer == 0, 0.0, 1.0)

    def store(comp, i, j, value):
        full[spot(comp, i, j), :] = value * off_wall if i == 0 else value

    join_step(width_ref[0], near, far, own, sides, state, store)
    out[...] = full[...].astype(BF16)
    along = 2.0 / jnp.full((8, 128), height_ref[0], F32)
    for j in range(NODES):
        rows = weighted(DERIV[0], [full[spot(0, i, j), :] for i in range(NODES)])
        rows = (WALL_GAIN * along) * rows * mask_ref[0, j].astype(F32)
        wall[pl.ds(j, 1), :] = rows[0:1]


def ring(value, shift):
    count = lax.axis_size("xsec")
    return lax.ppermute(value, "xsec", [(n, (n + shift) % count) for n in range(count)])


def swap(value, flip):
    return lax.ppermute(value, "span", [(n, n ^ flip) for n in range(lax.axis_size("span"))])


def halo(right, left, right_far, left_far):
    from_left, from_right = ring(right, 1), ring(left, -1)
    far_left, far_right = ring(right_far, 2), ring(left_far, -2)
    return from_left, from_right, far_left, far_right


def local(fwd_modes, adj_modes, layer_height, column_width, wall_mask):
    synth, wave, slope, analysis, kappa = plane_tables()
    kappa = jnp.asarray(kappa)
    pos = lax.axis_index("span").astype(jnp.int32).reshape(1)

    def resident(field):
        return field.transpose(0, 1, 3, 4, 2, 5).reshape(POINTS, 128)

    fwd_flat, adj_flat = resident(fwd_modes), resident(adj_modes)
    state_shapes = [((POINTS, 128), F32)]
    far_shapes = [((224, 128), BF16)] * 2
    work = [
        pltpu.VMEM((POINTS, 128), F32),
        pltpu.VMEM((PLANE * 8, 128), F32),
        pltpu.VMEM((2 * COLS * 8, 128), F32),
    ]

    adj_own, *adj_away = repack(pos, adj_flat, "adj_groups")
    adj_all = [adj_own] + [swap(part, flip + 1) for flip, part in enumerate(adj_away)]
    fwd_own, *fwd_away = repack(pos, fwd_flat, "fwd_groups")
    fwd_all = [fwd_own] + [swap(part, flip + 1) for flip, part in enumerate(fwd_away)]

    state, right, left, right_far, left_far = call(
        first_kernel,
        "first_substep",
        state_shapes + [((16 * COLS + 16, 128), BF16)] * 2 + far_shapes,
        work,
        [smem(), smem(), smem(), vmem(), vmem()],
        50_000_000,
        3_000_000,
    )(pos, layer_height, column_width, kappa, adj_flat)
    got = halo(right, left, right_far, left_far)

    parts = forcing(
        pos, layer_height, column_width, fwd_all, adj_all, (synth, wave, slope, analysis)
    )
    parts = [parts[0]] + [swap(part, flip + 1) for flip, part in enumerate(parts[1:])]

    base, sides = call(
        first_join_kernel,
        "first_join",
        state_shapes + [((16, 128), F32)],
        [],
        [smem()] + [vmem()] * 7,
        10_000_000,
        3_000_000,
    )(column_width, *got, right, left, state)

    state, right, left, right_far, left_far = call(
        second_kernel,
        "second_substep",
        state_shapes + [((16 * COLS, 128), BF16)] * 2 + far_shapes,
        [pltpu.VMEM((POINTS, 128), F32)] + work,
        [smem(), smem(), smem()] + [vmem()] * 6,
        50_000_000,
        4_000_000,
    )(pos, layer_height, column_width, kappa, base, *parts)
    got = halo(right, left, right_far, left_far)

    adj_new, wall = call(
        second_join_kernel,
        "second_join",
        [((POINTS, 128), BF16), ((NODES, 128), F32)],
        [pltpu.VMEM((POINTS, 128), F32)],
        [smem()] * 3 + [vmem()] * 8,
        10_000_000,
        3_000_000,
    )(column_width, layer_height, wall_mask, *got, right, left, sides, state)
    adj_new = adj_new.reshape(3, 1, NODES, NODES, 8, 128).transpose(0, 1, 4, 2, 3, 5)
    return adj_new, wall.reshape(1, NODES, 128)


def solution(mesh):
    return jax.shard_map(
        local,
        mesh=mesh,
        in_specs=(
            P(None, "xsec", None, None, None, "span"),
            P(None, "xsec", None, None, None, "span"),
            P(),
            P("xsec"),
            P("xsec", None),
        ),
        out_specs=(P(None, "xsec", None, None, None, "span"), P("xsec", None, "span")),
        check_vma=False,
    )
```

```python
import functools

import jax
import jax.numpy as jnp
import numpy as np
from jax import lax
from jax.experimental import pallas as pl
from jax.experimental.pallas import tpu as pltpu
from jax.sharding import PartitionSpec as P

NODES = 9
NK = 512
ADV_STEP = 0.0025
DIFFUSE = 5e-05
WALL_GAIN = 0.01
SPAN_GAIN = 1.0 / 32.0
PLANE = NODES * NODES
PAD = 88
ROWS = 3 * 2 * PAD
POINTS = 3 * PLANE * 8
COLS = 3 * NODES
F32 = jnp.float32
BF16 = jnp.bfloat16
MIB = 1 << 20


def cheb_table(number):
    degree = number - 1
    points = -np.cos(np.pi * np.arange(number) / degree)
    factor = np.where((np.arange(number) == 0) | (np.arange(number) == degree), 2.0, 1.0)
    parity = (-1.0) ** np.arange(number)
    spacing = points[:, None] - points[None, :] + np.eye(number)
    matrix = factor[:, None] * parity[:, None] * parity[None, :] / (factor[None, :] * spacing)
    matrix = matrix * (1.0 - np.eye(number))
    matrix = matrix - np.eye(number) * np.sum(matrix, axis=1)[:, None]
    return matrix.astype(np.float32)


def span_tables(modes):
    indices = np.arange(modes)
    pair_index = indices // 2
    wavenum = np.where(indices == 1, modes // 2, pair_index)
    planes = np.arange(modes)
    phases = 2.0 * np.pi * (wavenum[:, None] * planes[None, :] % modes) / modes
    basis_rows = np.where((indices % 2 == 0)[:, None], np.cos(phases), np.sin(phases))
    basis_rows = np.where((indices <= 1)[:, None], np.cos(phases), basis_rows)
    norm_gain = 1.0 / np.sqrt(modes / 2.0)
    weights_k = np.where(indices <= 1, 1.0, 2.0)
    synthesis = (basis_rows * norm_gain).astype(np.float32)
    analysis = ((basis_rows * (weights_k / (modes * norm_gain))[:, None]).T).astype(np.float32)
    slopes = np.where(indices <= 1, 0.0, pair_index * SPAN_GAIN).astype(np.float32)
    kappa_sq = ((wavenum * SPAN_GAIN) ** 2).astype(np.float32)
    return synthesis, analysis, slopes, kappa_sq


def halves(table):
    high = table.astype(jnp.bfloat16)
    return high, (table.astype(np.float64) - high.astype(np.float64)).astype(jnp.bfloat16)


DERIV = cheb_table(NODES).astype(np.float64)
INNER = DERIV[:, 1:8] @ DERIV[1:8, :]
FACED = INNER + 0.5 * np.outer(DERIV[:, 0], DERIV[0]) + 0.5 * np.outer(DERIV[:, 8], DERIV[8])


def plane_tables():
    synthesis, analysis, slopes, kappa_sq = span_tables(NK)
    wave = np.zeros((NK, NK))
    wave[1::2] = slopes[0::2, None].astype(np.float64) * synthesis[0::2]
    wave[0::2] = -slopes[1::2, None].astype(np.float64) * synthesis[1::2]
    radial = np.kron(DERIV, np.eye(NODES))
    around = np.kron(np.eye(NODES), DERIV)
    both = np.zeros((2, 2, PAD, 2, PAD))
    for layer in range(2):
        both[0, layer, :PLANE, layer, :PLANE] = radial
        both[1, layer, :PLANE, layer, :PLANE] = around
    high, low = halves(both.reshape(4 * PAD, 2 * PAD))
    slope = np.concatenate([high, low, high], axis=1)
    return synthesis.astype(jnp.bfloat16), halves(wave), slope, halves(analysis)


def smem():
    return pl.BlockSpec(memory_space=pltpu.SMEM)


def vmem():
    return pl.BlockSpec(memory_space=pltpu.VMEM)


def hbm():
    return pl.BlockSpec(memory_space=pltpu.HBM)


def in_hbm(value):
    return pltpu.with_memory_space_constraint(value, pltpu.HBM)


def call(kernel, name, outs, scratch, specs, flops, nbytes, mib):
    return pl.pallas_call(
        kernel,
        out_shape=[jax.ShapeDtypeStruct(shape, kind) for shape, kind in outs],
        in_specs=specs,
        out_specs=[vmem() for _ in outs],
        scratch_shapes=scratch,
        compiler_params=pltpu.CompilerParams(vmem_limit_bytes=mib * MIB),
        cost_estimate=pl.CostEstimate(flops=flops, bytes_accessed=nbytes, transcendentals=0),
        name=name,
    )


def repack_kernel(pos_ref, width_ref, adj_hbm, fwd_hbm, height_hbm, mask_hbm, *refs):
    groups, wide_adj, shape_ref = refs[0:4], refs[4], refs[5]
    adj_ref, fwd_ref, wide_fwd, height_ref, mask_ref, sems = refs[6:12]
    pairs = (
        (adj_hbm, adj_ref),
        (fwd_hbm, fwd_ref),
        (height_hbm, height_ref),
        (mask_hbm, mask_ref),
    )
    copies = [
        pltpu.make_async_copy(source, target, sems.at[n])
        for n, (source, target) in enumerate(pairs)
    ]
    for copy in copies:
        copy.start()
    pos = pos_ref[0]
    keep = lax.broadcasted_iota(jnp.int32, (PAD, 128), 0) < PLANE
    for which, (x_ref, wide) in enumerate(((adj_ref, wide_adj), (fwd_ref, wide_fwd))):
        copies[which].wait()
        wide[pl.ds(0, POINTS), :] = x_ref[...].astype(F32)
        for flip, out in enumerate(groups):
            group = pos ^ flip
            for comp in range(3):
                parts = []
                for layer in range(2):
                    start = comp * PLANE * 8 + 2 * group + layer
                    rows = wide[pl.ds(start, PAD, stride=8), :]
                    parts.append(jnp.where(keep, rows, 0.0))
                block = jnp.concatenate(parts, axis=0).astype(BF16)
                at = which * ROWS + comp * 2 * PAD
                out[at : at + 2 * PAD, :] = block
    for copy in copies[2:]:
        copy.wait()

    def spread(value):
        return jnp.full((8, 128), value, F32)

    layer = lax.broadcasted_iota(jnp.int32, (8, 128), 0)
    height = spread(height_ref[0])
    for index in range(1, 8):
        height = jnp.where(layer == index, height_ref[index], height)
    shape_ref[0:8, :] = 2.0 / height
    shape_ref[8:16, :] = 2.0 / spread(width_ref[0])
    shape_ref[16:24, :] = 2.0 / spread(height_ref[2 * pos])
    shape_ref[24:32, :] = 2.0 / spread(height_ref[2 * pos + 1])
    wall = WALL_GAIN * (2.0 / spread(height_ref[0]))
    for j in range(NODES):
        shape_ref[32 + 8 * j : 40 + 8 * j, :] = wall * mask_ref[0, j].astype(F32)


def repack(pos, adj, fwd, heights, widths, mask):
    return call(
        repack_kernel,
        "span_groups",
        [((2 * ROWS, 128), BF16)] * 4
        + [((POINTS + 56, 128), F32), ((32 + 8 * NODES, 128), F32)],
        [
            pltpu.VMEM((POINTS, 128), BF16),
            pltpu.VMEM((POINTS, 128), BF16),
            pltpu.VMEM((POINTS + 56, 128), F32),
            pltpu.SMEM((8,), F32),
            pltpu.SMEM((1, NODES), jnp.int32),
            pltpu.SemaphoreType.DMA((4,)),
        ],
        [smem()] * 2 + [hbm()] * 4,
        1_000_000,
        2_000_000,
        12,
    )(pos, widths, *map(in_hbm, (adj, fwd, heights, mask)))


def gather(ref, pos):
    parts = [ref[pl.ds(pl.multiple_of(128 * (pos ^ flip), 128), 128), :] for flip in range(4)]
    return jnp.concatenate(parts, axis=0)


def transform(pos, which, chunks, tables, planes, zplanes, grads):
    synth_ref, wave_hi_ref, wave_lo_ref, slope_ref = tables
    rows = slice(which * ROWS, (which + 1) * ROWS)
    modes = jnp.concatenate([chunk[rows, :] for chunk in chunks], axis=1)
    planes[...] = jnp.dot(modes, gather(synth_ref, pos), preferred_element_type=F32)
    zplanes[...] = jnp.dot(
        modes, gather(wave_hi_ref, pos), preferred_element_type=F32
    ) + jnp.dot(modes, gather(wave_lo_ref, pos), preferred_element_type=F32)
    slope = slope_ref[...]
    for comp in range(3):
        block = planes[comp * 2 * PAD : (comp + 1) * 2 * PAD, :]
        high = block.astype(BF16)
        low = (block - high.astype(F32)).astype(BF16)
        stack = jnp.concatenate([high, high, low], axis=0)
        grads[comp] = jnp.dot(slope, stack, preferred_element_type=F32)


def force_kernel(pos_ref, shape_ref, *refs):
    chunks, tables = refs[0:4], refs[4:10]
    outs = refs[10:14]
    adj_planes, adj_zplanes, adj_grads = refs[14:17]
    fwd_planes, fwd_zplanes, fwd_grads, force = refs[17:21]
    an_hi_ref, an_lo_ref = tables[4:]
    pos = pos_ref[0]
    transform(pos, 0, chunks, tables[:4], adj_planes, adj_zplanes, adj_grads)
    transform(pos, 1, chunks, tables[:4], fwd_planes, fwd_zplanes, fwd_grads)
    planes, zplanes = (fwd_planes, adj_planes), (fwd_zplanes, adj_zplanes)
    grads = (fwd_grads, adj_grads)

    across = shape_ref[8:16, :]
    for layer in range(2):
        along = shape_ref[16 + 8 * layer : 24 + 8 * layer, :]
        for tile in range(PAD // 8):
            row = layer * PAD + 8 * tile
            for lane in range(0, NK, 128):
                lanes = slice(lane, lane + 128)

                def plane(which, comp):
                    at = comp * 2 * PAD + row
                    return planes[which][at : at + 8, lanes]

                def zplane(which, comp):
                    at = comp * 2 * PAD + row
                    return zplanes[which][at : at + 8, lanes]

                def grad(which, direc, comp):
                    at = direc * 2 * PAD + row
                    return grads[which][comp, at : at + 8, lanes]

                fwd_r = plane(0, 0) * along
                fwd_t = plane(0, 1) * across
                fwd_z = plane(0, 2)
                adj_p = [plane(1, comp) for comp in range(3)]
                pulled = [
                    along * sum(adj_p[comp] * grad(0, 0, comp) for comp in range(3)),
                    across * sum(adj_p[comp] * grad(0, 1, comp) for comp in range(3)),
                    sum(adj_p[comp] * zplane(0, comp) for comp in range(3)),
                ]
                for comp in range(3):
                    carried = (
                        fwd_r * grad(1, 0, comp) + fwd_t * grad(1, 1, comp) + fwd_z * zplane(1, comp)
                    )
                    at = comp * 2 * PAD + row
                    force[at : at + 8, lanes] = carried - pulled[comp]

    def pick(ref):
        return jnp.concatenate([ref[pos ^ flip] for flip in range(4)], axis=1)

    an_hi, an_lo = pick(an_hi_ref), pick(an_lo_ref)
    total = force[...]
    high = total.astype(BF16)
    low = (total - high.astype(F32)).astype(BF16)
    result = (
        jnp.dot(high, an_hi, preferred_element_type=F32)
        + jnp.dot(low, an_hi, preferred_element_type=F32)
        + jnp.dot(high, an_lo, preferred_element_type=F32)
    ).astype(BF16)
    for flip, out in enumerate(outs):
        out[...] = result[:, 128 * flip : 128 * (flip + 1)]


def plane_shapes():
    return [(ROWS, NK), (ROWS, NK), (3, 4 * PAD, NK)]


def forcing(pos, shape, chunks, tables):
    fields = [pltpu.VMEM(shape, F32) for shape in plane_shapes()]
    return call(
        force_kernel,
        "adjoint_forcing",
        [((ROWS, 128), BF16)] * 4,
        fields + fields + [pltpu.VMEM((ROWS, NK), F32)],
        [smem()] + [vmem()] * 11,
        5_000_000_000,
        8_000_000,
        20,
    )(pos, shape, *chunks, *tables)


def mirror(matrix):
    even = np.concatenate(
        [0.5 * (matrix[:5, :4] + matrix[:5, :4:-1]), matrix[:5, 4:5]], axis=1
    )
    odd = 0.5 * (matrix[:4, :4] - matrix[:4, :4:-1])
    return even, odd


def weighted(coeffs, values):
    total = None
    for coeff, value in zip(coeffs, values):
        term = float(coeff) * value
        total = term if total is None else total + term
    return total


def parity(values):
    even = [values[n] + values[8 - n] for n in range(4)] + [values[4]]
    odd = [values[n] - values[8 - n] for n in range(4)]
    return even, odd


def ends(even, odd):
    row_even = np.concatenate([0.5 * (DERIV[0, :4] + DERIV[0, :4:-1]), DERIV[0, 4:5]])
    row_odd = 0.5 * (DERIV[0, :4] - DERIV[0, :4:-1])
    first, second = weighted(row_even, even), weighted(row_odd, odd)
    return second + first, second - first


def unfold(even, odd):
    low = [even[n] + odd[n] for n in range(4)]
    high = [even[n] - odd[n] for n in range(4)]
    return low + [even[4]] + high[::-1]


def wave_squares(pos):
    index = lax.broadcasted_iota(jnp.int32, (8, 128), 1) + 128 * pos
    wave = jnp.where(index == 1, NK // 2, index >> 1).astype(F32) * SPAN_GAIN
    return wave * wave


def layer_vectors(shape_ref):
    layer = lax.broadcasted_iota(jnp.int32, (8, 128), 0)
    along = shape_ref[0:8, :]
    below = pltpu.roll(along, 1, 0)
    above = pltpu.roll(along, 7, 0)
    bottom, top = layer == 0, layer == 7
    own_low = jnp.where(bottom, 1.0, 0.5)
    own_high = jnp.where(top, 1.0, 0.5)
    from_below = jnp.where(bottom, 0.0, 0.5)
    from_above = jnp.where(top, 0.0, 0.5)
    return dict(
        layer=layer,
        along=along,
        across=shape_ref[8:16, :],
        own_low=own_low,
        own_high=own_high,
        from_below=from_below,
        from_above=from_above,
        grad_below=from_below * below / along,
        grad_above=from_above * above / along,
    )


def local_step(vec, kappa, load, store, sent, two_away, visc, faces):
    across = vec["across"]
    scale_t = DIFFUSE * across * across
    scale_r = DIFFUSE * vec["along"] * vec["along"]
    scale_k = DIFFUSE * kappa
    even_t, odd_t = mirror(FACED)
    even_r, odd_r = mirror(INNER)
    mix_even = 0.5 * (DERIV[:5, 0] - DERIV[:5, 8])
    mix_odd = 0.5 * (DERIV[:4, 0] + DERIV[:4, 8])

    def shared(low, high):
        low_new = vec["own_low"] * low + vec["from_below"] * pltpu.roll(high, 1, 0)
        high_new = vec["own_high"] * high + vec["from_above"] * pltpu.roll(low, 7, 0)
        return low_new, high_new

    right_ref, left_ref = sent
    right_far, left_far = two_away

    for comp in range(3):
        edge_low, edge_high = [], []
        for i in range(NODES):
            values = [load(comp, i, j) for j in range(NODES)]
            even, odd = parity(values)
            low, high = ends(even, odd)
            edge_low.append(across * low)
            edge_high.append(across * high)
            even_out = [weighted(even_t[n], even) for n in range(5)]
            odd_out = [weighted(odd_t[n], odd) for n in range(4)]
            for j, value in enumerate(unfold(even_out, odd_out)):
                visc[pl.ds(8 * (i * NODES + j), 8), :] = scale_t * value
        for edge, ref in ((edge_low, 0), (edge_high, 1)):
            edge[0], edge[8] = shared(edge[0], edge[8])
            for i in range(NODES):
                faces[pl.ds(8 * ((ref * 3 + comp) * NODES + i), 8), :] = edge[i]
        for j in range(NODES):
            values = [load(comp, i, j) for i in range(NODES)]
            even, odd = parity(values)
            low, high = ends(even, odd)
            low_mean = vec["own_low"] * low + vec["grad_below"] * pltpu.roll(high, 1, 0)
            high_mean = vec["own_high"] * high + vec["grad_above"] * pltpu.roll(low, 7, 0)
            differ, total = low_mean - high_mean, low_mean + high_mean
            even_out = [
                weighted(even_r[n], even) + float(mix_even[n]) * differ for n in range(5)
            ]
            odd_out = [weighted(odd_r[n], odd) + float(mix_odd[n]) * total for n in range(4)]
            lap = [
                scale_r * value - scale_k * values[i] + visc[pl.ds(8 * (i * NODES + j), 8), :]
                for i, value in enumerate(unfold(even_out, odd_out))
            ]
            lap[0], lap[8] = shared(lap[0], lap[8])
            if j == 0 or j == 8:
                ref, side = (left_ref, 0) if j == 0 else (right_ref, 1)
                for i in range(NODES):
                    edge = faces[pl.ds(8 * ((side * 3 + comp) * NODES + i), 8), :]
                    pair = jnp.concatenate([edge, lap[i]], axis=0).astype(BF16)
                    ref[pl.ds(16 * (comp * NODES + i), 16), :] = pair
            for i in range(NODES):
                step = 0.5 * lap[i] if j == 0 or j == 8 else lap[i]
                store(comp, i, j, values[i], step)
    for side, ref in ((0, left_far), (1, right_far)):
        for block in range(14):
            first = faces[pl.ds(8 * (side * COLS + 2 * block), 8), :]
            if 2 * block + 1 < COLS:
                second = faces[pl.ds(8 * (side * COLS + 2 * block + 1), 8), :]
            else:
                second = jnp.zeros((8, 128), F32)
            ref[pl.ds(16 * block, 16), :] = jnp.concatenate([first, second], axis=0).astype(BF16)


def spot(comp, i, j):
    return pl.ds(8 * ((comp * NODES + i) * NODES + j), 8)


def first_kernel(pos_ref, shape_ref, wide, *refs):
    given, refs = refs[0:6], refs[6:]
    out, right, left, right_far, left_far = refs[0:5]
    tables, (visc, faces, sems) = refs[5:11], refs[11:14]
    copies = [
        pltpu.make_async_copy(source, target, sems.at[n])
        for n, (source, target) in enumerate(zip(given, tables))
    ]
    for copy in copies:
        copy.start()

    def load(comp, i, j):
        return wide[spot(comp, i, j), :]

    def store(comp, i, j, value, step):
        out[spot(comp, i, j), :] = value + step

    vec = layer_vectors(shape_ref)
    kappa = wave_squares(pos_ref[0])
    local_step(vec, kappa, load, store, (right, left), (right_far, left_far), visc, faces)
    across = vec["across"]
    high = across.astype(BF16).astype(F32)
    mid = (across - high).astype(BF16).astype(F32)
    low = across - high - mid
    layer = vec["layer"]
    note = jnp.where(layer == 0, high, jnp.where(layer == 1, mid, jnp.where(layer == 2, low, 0.0)))
    block = jnp.concatenate([note, jnp.zeros((8, 128), F32)], axis=0).astype(BF16)
    for ref in (right, left):
        ref[pl.ds(16 * COLS, 16), :] = block
    for copy in copies:
        copy.wait()


def second_kernel(pos_ref, shape_ref, base_ref, *refs):
    chunks = refs[:4]
    out, right, left, right_far, left_far, push, wide, visc, faces = refs[4:]
    pos = pos_ref[0]
    for flip, chunk in enumerate(chunks):
        group = pos ^ flip
        for comp in range(3):
            block = ADV_STEP * chunk[comp * 2 * PAD : (comp + 1) * 2 * PAD, :].astype(F32)
            for layer in range(2):
                start = comp * PLANE * 8 + 2 * group + layer
                push[pl.ds(start, PLANE, stride=8), :] = block[layer * PAD : layer * PAD + PLANE]
    vec = layer_vectors(shape_ref)
    off_wall = jnp.where(vec["layer"] == 0, 0.0, 1.0)
    for comp in range(3):
        for i in range(NODES):
            for j in range(NODES):
                at = spot(comp, i, j)
                value = base_ref[at, :] + push[at, :]
                wide[at, :] = value * off_wall if i == 0 else value

    def load(comp, i, j):
        return wide[spot(comp, i, j), :]

    def store(comp, i, j, value, step):
        at = spot(comp, i, j)
        out[at, :] = value + push[at, :] + step

    local_step(
        vec,
        wave_squares(pos),
        load,
        store,
        (right, left),
        (right_far, left_far),
        visc,
        faces,
    )


def join_step(shape_ref, near, far, own, sides, state, store):
    from_left, from_right = near
    far_left, far_right = far
    own_right, own_left = own
    across = shape_ref[8:16, :]
    gain = (0.5 * DIFFUSE) * across
    gain_left, gain_right = (0.5 * DIFFUSE) * sides[0], (0.5 * DIFFUSE) * sides[1]
    for block in range(14):
        far_l = far_left[pl.ds(16 * block, 16), :].astype(F32)
        far_r = far_right[pl.ds(16 * block, 16), :].astype(F32)
        for half in range(2):
            col = 2 * block + half
            if col >= COLS:
                continue
            comp, i = divmod(col, NODES)
            at = pl.ds(16 * col, 16)
            pair_l, pair_r = from_left[at, :].astype(F32), from_right[at, :].astype(F32)
            mine_low = own_left[at, :].astype(F32)[0:8]
            mine_high = own_right[at, :].astype(F32)[0:8]
            grad_l, grad_r = gain * pair_l[0:8], gain * pair_r[0:8]
            two_l, two_r = far_l[8 * half : 8 * half + 8], far_r[8 * half : 8 * half + 8]
            for j in range(NODES):
                add = float(DERIV[j, 0]) * grad_l + float(DERIV[j, 8]) * grad_r
                if j == 0:
                    other = gain_left * (float(DERIV[8, 0]) * two_l + float(DERIV[8, 8]) * mine_low)
                    add = 0.5 * (add + pair_l[8:16] + other)
                if j == 8:
                    other = gain_right * (float(DERIV[0, 0]) * mine_high + float(DERIV[0, 8]) * two_r)
                    add = 0.5 * (add + pair_r[8:16] + other)
                store(comp, i, j, state[spot(comp, i, j), :] + add)


def first_join_kernel(shape_ref, *refs):
    near, far, own = refs[0:2], refs[2:4], refs[4:6]
    state, out, sides_out = refs[6:9]
    sides = []
    for side, ref in enumerate(near):
        note = ref[pl.ds(16 * COLS, 16), :].astype(F32)[0:8]
        value = jnp.broadcast_to(jnp.sum(note, axis=0, keepdims=True), (8, 128))
        sides_out[pl.ds(8 * side, 8), :] = value
        sides.append(value)

    def store(comp, i, j, value):
        out[spot(comp, i, j), :] = value

    join_step(shape_ref, near, far, own, sides, state, store)


def second_join_kernel(shape_ref, *refs):
    near, far, own = refs[0:2], refs[2:4], refs[4:6]
    sides_ref, state, out, wall, full = refs[6:11]
    sides = [sides_ref[pl.ds(0, 8), :], sides_ref[pl.ds(8, 8), :]]
    layer = lax.broadcasted_iota(jnp.int32, (8, 128), 0)
    off_wall = jnp.where(layer == 0, 0.0, 1.0)

    def store(comp, i, j, value):
        full[spot(comp, i, j), :] = value * off_wall if i == 0 else value

    join_step(shape_ref, near, far, own, sides, state, store)
    out[...] = full[...].astype(BF16)
    for j in range(NODES):
        rows = weighted(DERIV[0], [full[spot(0, i, j), :] for i in range(NODES)])
        rows = rows * shape_ref[pl.ds(32 + 8 * j, 8), :]
        wall[j] = rows[0:1]


def ring(value, shift):
    count = lax.axis_size("xsec")
    return lax.ppermute(value, "xsec", [(n, (n + shift) % count) for n in range(count)])


def swap(value, flip):
    return lax.ppermute(value, "span", [(n, n ^ flip) for n in range(lax.axis_size("span"))])


def halo(right, left, shift):
    return [ring(right, shift), ring(left, -shift)]


def local(fwd_modes, adj_modes, layer_height, column_width, wall_mask):
    synth, (wave_hi, wave_lo), slope, (an_hi, an_lo) = plane_tables()
    split = lambda table: table.reshape(NK, 4, 128).transpose(1, 0, 2)
    constants = [
        jnp.asarray(table)
        for table in (synth, wave_hi, wave_lo, slope, split(an_hi), split(an_lo))
    ]
    pos = lax.axis_index("span").astype(jnp.int32).reshape(1)

    def resident(field):
        return field.transpose(0, 1, 3, 4, 2, 5).reshape(POINTS, 128)

    fwd_flat, adj_flat = resident(fwd_modes), resident(adj_modes)
    state_shape = ((POINTS, 128), F32)
    far_shapes = [((224, 128), BF16)] * 2
    work = [pltpu.VMEM((PLANE * 8, 128), F32), pltpu.VMEM((2 * COLS * 8, 128), F32)]

    def exchange(parts):
        return [parts[0]] + [swap(part, flip + 1) for flip, part in enumerate(parts[1:])]

    *groups, adj_wide, shape = repack(
        pos, adj_flat, fwd_flat, layer_height, column_width, wall_mask
    )
    chunks = exchange(groups)

    state, right, left, right_far, left_far, *tables = call(
        first_kernel,
        "first_substep",
        [state_shape]
        + [((16 * COLS + 16, 128), BF16)] * 2
        + far_shapes
        + [(table.shape, BF16) for table in constants],
        work + [pltpu.SemaphoreType.DMA((6,))],
        [smem()] + [vmem()] * 2 + [hbm()] * 6,
        50_000_000,
        3_000_000,
        10,
    )(pos, shape, adj_wide, *map(in_hbm, constants))
    near, far = halo(right, left, 1), halo(right_far, left_far, 2)
    *far, chunks[0] = lax.optimization_barrier((*far, chunks[0]))
    parts = forcing(pos, shape, chunks, tables)
    *near, parts = lax.optimization_barrier((*near, tuple(parts)))
    parts = exchange(parts)

    base, sides = call(
        first_join_kernel,
        "first_join",
        [state_shape, ((16, 128), F32)],
        [],
        [vmem()] * 8,
        10_000_000,
        3_000_000,
        8,
    )(shape, *near, *far, right, left, state)

    state, right, left, right_far, left_far = call(
        second_kernel,
        "second_substep",
        [state_shape] + [((16 * COLS, 128), BF16)] * 2 + far_shapes,
        [pltpu.VMEM((POINTS, 128), F32)] * 2 + work,
        [smem()] + [vmem()] * 6,
        50_000_000,
        4_000_000,
        12,
    )(pos, shape, base, *parts)
    got = halo(right, left, 1) + halo(right_far, left_far, 2)

    adj_new, wall = call(
        second_join_kernel,
        "second_join",
        [((POINTS, 128), BF16), ((NODES, 1, 128), F32)],
        [pltpu.VMEM((POINTS, 128), F32)],
        [vmem()] * 9,
        10_000_000,
        3_000_000,
        8,
    )(shape, *got, right, left, sides, state)
    adj_new = adj_new.reshape(3, 1, NODES, NODES, 8, 128).transpose(0, 1, 4, 2, 3, 5)
    return adj_new, wall.transpose(1, 0, 2)


def solution(mesh):
    return jax.shard_map(
        local,
        mesh=mesh,
        in_specs=(
            P(None, "xsec", None, None, None, "span"),
            P(None, "xsec", None, None, None, "span"),
            P(),
            P("xsec"),
            P("xsec", None),
        ),
        out_specs=(P(None, "xsec", None, None, None, "span"), P("xsec", None, "span")),
        check_vma=False,
    )
```

```python
import functools

import jax
import jax.numpy as jnp
import numpy as np
from jax import lax
from jax.experimental import pallas as pl
from jax.experimental.pallas import tpu as pltpu
from jax.sharding import PartitionSpec as P

NODES = 9
NK = 512
ADV_STEP = 0.0025
DIFFUSE = 5e-05
WALL_GAIN = 0.01
SPAN_GAIN = 1.0 / 32.0
PLANE = NODES * NODES
PAD = 88
ROWS = 3 * 2 * PAD
POINTS = 3 * PLANE * 8
COLS = 3 * NODES
F32 = jnp.float32
BF16 = jnp.bfloat16
MIB = 1 << 20


def cheb_table(number):
    degree = number - 1
    points = -np.cos(np.pi * np.arange(number) / degree)
    factor = np.where((np.arange(number) == 0) | (np.arange(number) == degree), 2.0, 1.0)
    parity = (-1.0) ** np.arange(number)
    spacing = points[:, None] - points[None, :] + np.eye(number)
    matrix = factor[:, None] * parity[:, None] * parity[None, :] / (factor[None, :] * spacing)
    matrix = matrix * (1.0 - np.eye(number))
    matrix = matrix - np.eye(number) * np.sum(matrix, axis=1)[:, None]
    return matrix.astype(np.float32)


def span_tables(modes):
    indices = np.arange(modes)
    pair_index = indices // 2
    wavenum = np.where(indices == 1, modes // 2, pair_index)
    planes = np.arange(modes)
    phases = 2.0 * np.pi * (wavenum[:, None] * planes[None, :] % modes) / modes
    basis_rows = np.where((indices % 2 == 0)[:, None], np.cos(phases), np.sin(phases))
    basis_rows = np.where((indices <= 1)[:, None], np.cos(phases), basis_rows)
    norm_gain = 1.0 / np.sqrt(modes / 2.0)
    weights_k = np.where(indices <= 1, 1.0, 2.0)
    synthesis = (basis_rows * norm_gain).astype(np.float32)
    analysis = ((basis_rows * (weights_k / (modes * norm_gain))[:, None]).T).astype(np.float32)
    slopes = np.where(indices <= 1, 0.0, pair_index * SPAN_GAIN).astype(np.float32)
    kappa_sq = ((wavenum * SPAN_GAIN) ** 2).astype(np.float32)
    return synthesis, analysis, slopes, kappa_sq


def halves(table):
    high = table.astype(jnp.bfloat16)
    return high, (table.astype(np.float64) - high.astype(np.float64)).astype(jnp.bfloat16)


DERIV = cheb_table(NODES).astype(np.float64)
INNER = DERIV[:, 1:8] @ DERIV[1:8, :]
FACED = INNER + 0.5 * np.outer(DERIV[:, 0], DERIV[0]) + 0.5 * np.outer(DERIV[:, 8], DERIV[8])


def plane_tables():
    synthesis, analysis, slopes, kappa_sq = span_tables(NK)
    wave = np.zeros((NK, NK))
    wave[1::2] = slopes[0::2, None].astype(np.float64) * synthesis[0::2]
    wave[0::2] = -slopes[1::2, None].astype(np.float64) * synthesis[1::2]
    radial = np.kron(DERIV, np.eye(NODES))
    around = np.kron(np.eye(NODES), DERIV)
    both = np.zeros((2, 2, PAD, 2, PAD))
    for layer in range(2):
        both[0, layer, :PLANE, layer, :PLANE] = radial
        both[1, layer, :PLANE, layer, :PLANE] = around
    high, low = halves(both.reshape(4 * PAD, 2 * PAD))
    slope = np.concatenate([high, low], axis=1)
    kinds = [table.astype(jnp.bfloat16) for table in (synthesis, wave, analysis)]
    return kinds[0], kinds[1], slope, kinds[2]


def smem():
    return pl.BlockSpec(memory_space=pltpu.SMEM)


def vmem():
    return pl.BlockSpec(memory_space=pltpu.VMEM)


def hbm():
    return pl.BlockSpec(memory_space=pltpu.HBM)


def in_hbm(value):
    return pltpu.with_memory_space_constraint(value, pltpu.HBM)


def call(kernel, name, outs, scratch, specs, flops, nbytes, mib):
    return pl.pallas_call(
        kernel,
        out_shape=[jax.ShapeDtypeStruct(shape, kind) for shape, kind in outs],
        in_specs=specs,
        out_specs=[vmem() for _ in outs],
        scratch_shapes=scratch,
        compiler_params=pltpu.CompilerParams(vmem_limit_bytes=mib * MIB),
        cost_estimate=pl.CostEstimate(flops=flops, bytes_accessed=nbytes, transcendentals=0),
        name=name,
    )


def repack_kernel(pos_ref, width_ref, adj_hbm, fwd_hbm, height_hbm, mask_hbm, *refs):
    shared, adj_single, fwd_single = refs[0:2], refs[2:4], refs[4:6]
    wide_adj, shape_ref = refs[6:8]
    adj_ref, fwd_ref, wide_fwd, height_ref, mask_ref, sems = refs[8:14]
    singles = (adj_single, fwd_single)
    pairs = (
        (adj_hbm, adj_ref),
        (fwd_hbm, fwd_ref),
        (height_hbm, height_ref),
        (mask_hbm, mask_ref),
    )
    copies = [
        pltpu.make_async_copy(source, target, sems.at[n])
        for n, (source, target) in enumerate(pairs)
    ]
    for copy in copies:
        copy.start()
    pos = pos_ref[0]
    keep = lax.broadcasted_iota(jnp.int32, (PAD, 128), 0) < PLANE
    for which, (x_ref, wide) in enumerate(((adj_ref, wide_adj), (fwd_ref, wide_fwd))):
        copies[which].wait()
        wide[pl.ds(0, POINTS), :] = x_ref[...].astype(F32)
        for flip, out in enumerate((*shared, *singles[which])):
            group = pos ^ flip
            for comp in range(3):
                parts = []
                for layer in range(2):
                    start = comp * PLANE * 8 + 2 * group + layer
                    rows = wide[pl.ds(start, PAD, stride=8), :]
                    parts.append(jnp.where(keep, rows, 0.0))
                block = jnp.concatenate(parts, axis=0).astype(BF16)
                at = comp * 2 * PAD + (which * ROWS if flip < 2 else 0)
                out[at : at + 2 * PAD, :] = block
    for copy in copies[2:]:
        copy.wait()

    def spread(value):
        return jnp.full((8, 128), value, F32)

    layer = lax.broadcasted_iota(jnp.int32, (8, 128), 0)
    height = spread(height_ref[0])
    for index in range(1, 8):
        height = jnp.where(layer == index, height_ref[index], height)
    shape_ref[0:8, :] = 2.0 / height
    shape_ref[8:16, :] = 2.0 / spread(width_ref[0])
    shape_ref[16:24, :] = 2.0 / spread(height_ref[2 * pos])
    shape_ref[24:32, :] = 2.0 / spread(height_ref[2 * pos + 1])
    wall = WALL_GAIN * (2.0 / spread(height_ref[0]))
    for j in range(NODES):
        shape_ref[32 + 8 * j : 40 + 8 * j, :] = wall * mask_ref[0, j].astype(F32)


def repack(pos, adj, fwd, heights, widths, mask):
    return call(
        repack_kernel,
        "span_groups",
        [((2 * ROWS, 128), BF16)] * 2
        + [((ROWS, 128), BF16)] * 4
        + [((POINTS + 56, 128), F32), ((32 + 8 * NODES, 128), F32)],
        [
            pltpu.VMEM((POINTS, 128), BF16),
            pltpu.VMEM((POINTS, 128), BF16),
            pltpu.VMEM((POINTS + 56, 128), F32),
            pltpu.SMEM((8,), F32),
            pltpu.SMEM((1, NODES), jnp.int32),
            pltpu.SemaphoreType.DMA((4,)),
        ],
        [smem()] * 2 + [hbm()] * 4,
        1_000_000,
        2_000_000,
        12,
    )(pos, widths, *map(in_hbm, (adj, fwd, heights, mask)))


def gather(ref, pos):
    parts = [ref[pl.ds(pl.multiple_of(128 * (pos ^ flip), 128), 128), :] for flip in range(4)]
    return jnp.concatenate(parts, axis=0)


def transform(pos, which, shared, single, tables, planes, zplanes, grads):
    synth_ref, wave_ref, slope_ref = tables
    rows = slice(which * ROWS, (which + 1) * ROWS)
    parts = [chunk[rows, :] for chunk in shared] + [chunk[...] for chunk in single]
    modes = jnp.concatenate(parts, axis=1)
    planes[...] = jnp.dot(modes, gather(synth_ref, pos), preferred_element_type=F32)
    zplanes[...] = jnp.dot(modes, gather(wave_ref, pos), preferred_element_type=F32)
    slope = slope_ref[...]
    for comp in range(3):
        block = planes[comp * 2 * PAD : (comp + 1) * 2 * PAD, :].astype(BF16)
        stack = jnp.concatenate([block, block], axis=0)
        grads[comp] = jnp.dot(slope, stack, preferred_element_type=F32)


def adj_kernel(pos_ref, *refs):
    transform(pos_ref[0], 0, refs[0:2], refs[2:4], refs[4:7], *refs[7:10])


def force_kernel(pos_ref, shape_ref, *refs):
    tables, an_ref = refs[4:7], refs[7]
    adj_planes, adj_zplanes, adj_grads = refs[8:11]
    outs = refs[11:15]
    fwd_planes, fwd_zplanes, fwd_grads, force = refs[15:19]
    pos = pos_ref[0]
    transform(pos, 1, refs[0:2], refs[2:4], tables, fwd_planes, fwd_zplanes, fwd_grads)
    planes, zplanes = (fwd_planes, adj_planes), (fwd_zplanes, adj_zplanes)
    grads = (fwd_grads, adj_grads)

    across = shape_ref[8:16, :]
    for layer in range(2):
        along = shape_ref[16 + 8 * layer : 24 + 8 * layer, :]
        for tile in range(PAD // 8):
            row = layer * PAD + 8 * tile
            for lane in range(0, NK, 128):
                lanes = slice(lane, lane + 128)

                def plane(which, comp):
                    at = comp * 2 * PAD + row
                    return planes[which][at : at + 8, lanes]

                def zplane(which, comp):
                    at = comp * 2 * PAD + row
                    return zplanes[which][at : at + 8, lanes]

                def grad(which, direc, comp):
                    at = direc * 2 * PAD + row
                    return grads[which][comp, at : at + 8, lanes]

                fwd_r = plane(0, 0) * along
                fwd_t = plane(0, 1) * across
                fwd_z = plane(0, 2)
                adj_p = [plane(1, comp) for comp in range(3)]
                pulled = [
                    along * sum(adj_p[comp] * grad(0, 0, comp) for comp in range(3)),
                    across * sum(adj_p[comp] * grad(0, 1, comp) for comp in range(3)),
                    sum(adj_p[comp] * zplane(0, comp) for comp in range(3)),
                ]
                for comp in range(3):
                    carried = (
                        fwd_r * grad(1, 0, comp) + fwd_t * grad(1, 1, comp) + fwd_z * zplane(1, comp)
                    )
                    at = comp * 2 * PAD + row
                    force[at : at + 8, lanes] = carried - pulled[comp]

    def pick(ref):
        return jnp.concatenate([ref[pos ^ flip] for flip in range(4)], axis=1)

    analysis = pick(an_ref)
    total = force[...]
    high = total.astype(BF16)
    low = (total - high.astype(F32)).astype(BF16)
    result = (
        jnp.dot(high, analysis, preferred_element_type=F32)
        + jnp.dot(low, analysis, preferred_element_type=F32)
    ).astype(BF16)
    for flip, out in enumerate(outs):
        out[...] = result[:, 128 * flip : 128 * (flip + 1)]


def plane_shapes():
    return [(ROWS, NK), (ROWS, NK), (3, 4 * PAD, NK)]


def adj_side(pos, shared, single, tables):
    return call(
        adj_kernel,
        "adjoint_planes",
        [(shape, F32) for shape in plane_shapes()],
        [],
        [smem()] + [vmem()] * 7,
        1_500_000_000,
        8_000_000,
        12,
    )(pos, *shared, *single, *tables)


def forcing(pos, shape, shared, single, tables, adj_fields):
    return call(
        force_kernel,
        "adjoint_forcing",
        [((ROWS, 128), BF16)] * 4,
        [pltpu.VMEM(dims, F32) for dims in plane_shapes()] + [pltpu.VMEM((ROWS, NK), F32)],
        [smem()] + [vmem()] * 12,
        2_500_000_000,
        8_000_000,
        20,
    )(pos, shape, *shared, *single, *tables, *adj_fields)


def mirror(matrix):
    even = np.concatenate(
        [0.5 * (matrix[:5, :4] + matrix[:5, :4:-1]), matrix[:5, 4:5]], axis=1
    )
    odd = 0.5 * (matrix[:4, :4] - matrix[:4, :4:-1])
    return even, odd


def weighted(coeffs, values):
    total = None
    for coeff, value in zip(coeffs, values):
        term = float(coeff) * value
        total = term if total is None else total + term
    return total


def parity(values):
    even = [values[n] + values[8 - n] for n in range(4)] + [values[4]]
    odd = [values[n] - values[8 - n] for n in range(4)]
    return even, odd


def ends(even, odd):
    row_even = np.concatenate([0.5 * (DERIV[0, :4] + DERIV[0, :4:-1]), DERIV[0, 4:5]])
    row_odd = 0.5 * (DERIV[0, :4] - DERIV[0, :4:-1])
    first, second = weighted(row_even, even), weighted(row_odd, odd)
    return second + first, second - first


def unfold(even, odd):
    low = [even[n] + odd[n] for n in range(4)]
    high = [even[n] - odd[n] for n in range(4)]
    return low + [even[4]] + high[::-1]


def wave_squares(pos):
    index = lax.broadcasted_iota(jnp.int32, (8, 128), 1) + 128 * pos
    wave = jnp.where(index == 1, NK // 2, index >> 1).astype(F32) * SPAN_GAIN
    return wave * wave


def layer_vectors(shape_ref):
    layer = lax.broadcasted_iota(jnp.int32, (8, 128), 0)
    along = shape_ref[0:8, :]
    below = pltpu.roll(along, 1, 0)
    above = pltpu.roll(along, 7, 0)
    bottom, top = layer == 0, layer == 7
    own_low = jnp.where(bottom, 1.0, 0.5)
    own_high = jnp.where(top, 1.0, 0.5)
    from_below = jnp.where(bottom, 0.0, 0.5)
    from_above = jnp.where(top, 0.0, 0.5)
    return dict(
        layer=layer,
        along=along,
        across=shape_ref[8:16, :],
        own_low=own_low,
        own_high=own_high,
        from_below=from_below,
        from_above=from_above,
        grad_below=from_below * below / along,
        grad_above=from_above * above / along,
    )


def local_step(vec, kappa, load, store, sent, two_away, visc, faces):
    across = vec["across"]
    scale_t = DIFFUSE * across * across
    scale_r = DIFFUSE * vec["along"] * vec["along"]
    scale_k = DIFFUSE * kappa
    even_t, odd_t = mirror(FACED)
    even_r, odd_r = mirror(INNER)
    mix_even = 0.5 * (DERIV[:5, 0] - DERIV[:5, 8])
    mix_odd = 0.5 * (DERIV[:4, 0] + DERIV[:4, 8])

    def shared(low, high):
        low_new = vec["own_low"] * low + vec["from_below"] * pltpu.roll(high, 1, 0)
        high_new = vec["own_high"] * high + vec["from_above"] * pltpu.roll(low, 7, 0)
        return low_new, high_new

    right_ref, left_ref = sent
    right_far, left_far = two_away

    for comp in range(3):
        edge_low, edge_high = [], []
        for i in range(NODES):
            values = [load(comp, i, j) for j in range(NODES)]
            even, odd = parity(values)
            low, high = ends(even, odd)
            edge_low.append(across * low)
            edge_high.append(across * high)
            even_out = [weighted(even_t[n], even) for n in range(5)]
            odd_out = [weighted(odd_t[n], odd) for n in range(4)]
            for j, value in enumerate(unfold(even_out, odd_out)):
                visc[pl.ds(8 * (i * NODES + j), 8), :] = scale_t * value
        for edge, ref in ((edge_low, 0), (edge_high, 1)):
            edge[0], edge[8] = shared(edge[0], edge[8])
            for i in range(NODES):
                faces[pl.ds(8 * ((ref * 3 + comp) * NODES + i), 8), :] = edge[i]
        for j in range(NODES):
            values = [load(comp, i, j) for i in range(NODES)]
            even, odd = parity(values)
            low, high = ends(even, odd)
            low_mean = vec["own_low"] * low + vec["grad_below"] * pltpu.roll(high, 1, 0)
            high_mean = vec["own_high"] * high + vec["grad_above"] * pltpu.roll(low, 7, 0)
            differ, total = low_mean - high_mean, low_mean + high_mean
            even_out = [
                weighted(even_r[n], even) + float(mix_even[n]) * differ for n in range(5)
            ]
            odd_out = [weighted(odd_r[n], odd) + float(mix_odd[n]) * total for n in range(4)]
            lap = [
                scale_r * value - scale_k * values[i] + visc[pl.ds(8 * (i * NODES + j), 8), :]
                for i, value in enumerate(unfold(even_out, odd_out))
            ]
            lap[0], lap[8] = shared(lap[0], lap[8])
            if j == 0 or j == 8:
                ref, side = (left_ref, 0) if j == 0 else (right_ref, 1)
                for i in range(NODES):
                    edge = faces[pl.ds(8 * ((side * 3 + comp) * NODES + i), 8), :]
                    pair = jnp.concatenate([edge, lap[i]], axis=0).astype(BF16)
                    ref[pl.ds(16 * (comp * NODES + i), 16), :] = pair
            for i in range(NODES):
                step = 0.5 * lap[i] if j == 0 or j == 8 else lap[i]
                store(comp, i, j, values[i], step)
    for side, ref in ((0, left_far), (1, right_far)):
        for block in range(14):
            first = faces[pl.ds(8 * (side * COLS + 2 * block), 8), :]
            if 2 * block + 1 < COLS:
                second = faces[pl.ds(8 * (side * COLS + 2 * block + 1), 8), :]
            else:
                second = jnp.zeros((8, 128), F32)
            ref[pl.ds(16 * block, 16), :] = jnp.concatenate([first, second], axis=0).astype(BF16)


def spot(comp, i, j):
    return pl.ds(8 * ((comp * NODES + i) * NODES + j), 8)


def first_kernel(pos_ref, shape_ref, wide, *refs):
    given, refs = refs[0:4], refs[4:]
    out, right, left, right_far, left_far = refs[0:5]
    tables, (visc, faces, sems) = refs[5:9], refs[9:12]
    copies = [
        pltpu.make_async_copy(source, target, sems.at[n])
        for n, (source, target) in enumerate(zip(given, tables))
    ]
    for copy in copies:
        copy.start()

    def load(comp, i, j):
        return wide[spot(comp, i, j), :]

    def store(comp, i, j, value, step):
        out[spot(comp, i, j), :] = value + step

    vec = layer_vectors(shape_ref)
    kappa = wave_squares(pos_ref[0])
    local_step(vec, kappa, load, store, (right, left), (right_far, left_far), visc, faces)
    across = vec["across"]
    high = across.astype(BF16).astype(F32)
    mid = (across - high).astype(BF16).astype(F32)
    low = across - high - mid
    layer = vec["layer"]
    note = jnp.where(layer == 0, high, jnp.where(layer == 1, mid, jnp.where(layer == 2, low, 0.0)))
    block = jnp.concatenate([note, jnp.zeros((8, 128), F32)], axis=0).astype(BF16)
    for ref in (right, left):
        ref[pl.ds(16 * COLS, 16), :] = block
    for copy in copies:
        copy.wait()


def second_kernel(pos_ref, shape_ref, base_ref, *refs):
    chunks = refs[:4]
    out, right, left, right_far, left_far, push, wide, visc, faces = refs[4:]
    pos = pos_ref[0]
    for flip, chunk in enumerate(chunks):
        group = pos ^ flip
        for comp in range(3):
            block = ADV_STEP * chunk[comp * 2 * PAD : (comp + 1) * 2 * PAD, :].astype(F32)
            for layer in range(2):
                start = comp * PLANE * 8 + 2 * group + layer
                push[pl.ds(start, PLANE, stride=8), :] = block[layer * PAD : layer * PAD + PLANE]
    vec = layer_vectors(shape_ref)
    off_wall = jnp.where(vec["layer"] == 0, 0.0, 1.0)
    for comp in range(3):
        for i in range(NODES):
            for j in range(NODES):
                at = spot(comp, i, j)
                value = base_ref[at, :] + push[at, :]
                wide[at, :] = value * off_wall if i == 0 else value

    def load(comp, i, j):
        return wide[spot(comp, i, j), :]

    def store(comp, i, j, value, step):
        at = spot(comp, i, j)
        out[at, :] = value + push[at, :] + step

    local_step(
        vec,
        wave_squares(pos),
        load,
        store,
        (right, left),
        (right_far, left_far),
        visc,
        faces,
    )


def join_step(shape_ref, near, far, own, sides, state, store):
    from_left, from_right = near
    far_left, far_right = far
    own_right, own_left = own
    across = shape_ref[8:16, :]
    gain = (0.5 * DIFFUSE) * across
    gain_left, gain_right = (0.5 * DIFFUSE) * sides[0], (0.5 * DIFFUSE) * sides[1]
    for block in range(14):
        far_l = far_left[pl.ds(16 * block, 16), :].astype(F32)
        far_r = far_right[pl.ds(16 * block, 16), :].astype(F32)
        for half in range(2):
            col = 2 * block + half
            if col >= COLS:
                continue
            comp, i = divmod(col, NODES)
            at = pl.ds(16 * col, 16)
            pair_l, pair_r = from_left[at, :].astype(F32), from_right[at, :].astype(F32)
            mine_low = own_left[at, :].astype(F32)[0:8]
            mine_high = own_right[at, :].astype(F32)[0:8]
            grad_l, grad_r = gain * pair_l[0:8], gain * pair_r[0:8]
            two_l, two_r = far_l[8 * half : 8 * half + 8], far_r[8 * half : 8 * half + 8]
            for j in range(NODES):
                add = float(DERIV[j, 0]) * grad_l + float(DERIV[j, 8]) * grad_r
                if j == 0:
                    other = gain_left * (float(DERIV[8, 0]) * two_l + float(DERIV[8, 8]) * mine_low)
                    add = 0.5 * (add + pair_l[8:16] + other)
                if j == 8:
                    other = gain_right * (float(DERIV[0, 0]) * mine_high + float(DERIV[0, 8]) * two_r)
                    add = 0.5 * (add + pair_r[8:16] + other)
                store(comp, i, j, state[spot(comp, i, j), :] + add)


def first_join_kernel(shape_ref, *refs):
    near, far, own = refs[0:2], refs[2:4], refs[4:6]
    state, out, sides_out = refs[6:9]
    sides = []
    for side, ref in enumerate(near):
        note = ref[pl.ds(16 * COLS, 16), :].astype(F32)[0:8]
        value = jnp.broadcast_to(jnp.sum(note, axis=0, keepdims=True), (8, 128))
        sides_out[pl.ds(8 * side, 8), :] = value
        sides.append(value)

    def store(comp, i, j, value):
        out[spot(comp, i, j), :] = value

    join_step(shape_ref, near, far, own, sides, state, store)


def second_join_kernel(shape_ref, *refs):
    near, far, own = refs[0:2], refs[2:4], refs[4:6]
    sides_ref, state, out, wall, full = refs[6:11]
    sides = [sides_ref[pl.ds(0, 8), :], sides_ref[pl.ds(8, 8), :]]
    layer = lax.broadcasted_iota(jnp.int32, (8, 128), 0)
    off_wall = jnp.where(layer == 0, 0.0, 1.0)

    def store(comp, i, j, value):
        full[spot(comp, i, j), :] = value * off_wall if i == 0 else value

    join_step(shape_ref, near, far, own, sides, state, store)
    out[...] = full[...].astype(BF16)
    for j in range(NODES):
        rows = weighted(DERIV[0], [full[spot(0, i, j), :] for i in range(NODES)])
        rows = rows * shape_ref[pl.ds(32 + 8 * j, 8), :]
        wall[j] = rows[0:1]


def ring(value, shift):
    count = lax.axis_size("xsec")
    return lax.ppermute(value, "xsec", [(n, (n + shift) % count) for n in range(count)])


def swap(value, flip):
    return lax.ppermute(value, "span", [(n, n ^ flip) for n in range(lax.axis_size("span"))])


def halo(right, left, shift):
    return [ring(right, shift), ring(left, -shift)]


def local(fwd_modes, adj_modes, layer_height, column_width, wall_mask):
    synth, wave, slope, analysis = plane_tables()
    analysis = analysis.reshape(NK, 4, 128).transpose(1, 0, 2)
    constants = [jnp.asarray(table) for table in (synth, wave, slope, analysis)]
    pos = lax.axis_index("span").astype(jnp.int32).reshape(1)

    def resident(field):
        return field.transpose(0, 1, 3, 4, 2, 5).reshape(POINTS, 128)

    fwd_flat, adj_flat = resident(fwd_modes), resident(adj_modes)
    state_shape = ((POINTS, 128), F32)
    far_shapes = [((224, 128), BF16)] * 2
    work = [pltpu.VMEM((PLANE * 8, 128), F32), pltpu.VMEM((2 * COLS * 8, 128), F32)]

    def exchange(parts):
        return [parts[0]] + [swap(part, flip + 1) for flip, part in enumerate(parts[1:])]

    own, sibling, adj_2, adj_3, fwd_2, fwd_3, adj_wide, shape = repack(
        pos, adj_flat, fwd_flat, layer_height, column_width, wall_mask
    )
    shared = [own, swap(sibling, 1)]
    adj_away, fwd_away = [swap(adj_2, 2), swap(adj_3, 3)], [swap(fwd_2, 2), swap(fwd_3, 3)]

    state, right, left, right_far, left_far, *tables = call(
        first_kernel,
        "first_substep",
        [state_shape]
        + [((16 * COLS + 16, 128), BF16)] * 2
        + far_shapes
        + [(table.shape, BF16) for table in constants],
        work + [pltpu.SemaphoreType.DMA((4,))],
        [smem()] + [vmem()] * 2 + [hbm()] * 4,
        50_000_000,
        3_000_000,
        10,
    )(pos, shape, adj_wide, *map(in_hbm, constants))
    near_right, near_left, *adj_away = lax.optimization_barrier((right, left, *adj_away))
    near = halo(near_right, near_left, 1)
    adj_fields = adj_side(pos, shared, adj_away, tables[:3])
    parts = forcing(pos, shape, shared, fwd_away, tables, adj_fields)
    parts = list(parts)
    right_far, left_far, *near, parts[0] = lax.optimization_barrier(
        (right_far, left_far, *near, parts[0])
    )
    parts = exchange(parts)
    far = halo(right_far, left_far, 2)

    base, sides = call(
        first_join_kernel,
        "first_join",
        [state_shape, ((16, 128), F32)],
        [],
        [vmem()] * 8,
        10_000_000,
        3_000_000,
        8,
    )(shape, *near, *far, right, left, state)

    state, right, left, right_far, left_far = call(
        second_kernel,
        "second_substep",
        [state_shape] + [((16 * COLS, 128), BF16)] * 2 + far_shapes,
        [pltpu.VMEM((POINTS, 128), F32)] * 2 + work,
        [smem()] + [vmem()] * 6,
        50_000_000,
        4_000_000,
        12,
    )(pos, shape, base, *parts)
    got = halo(right, left, 1) + halo(right_far, left_far, 2)

    adj_new, wall = call(
        second_join_kernel,
        "second_join",
        [((POINTS, 128), BF16), ((NODES, 1, 128), F32)],
        [pltpu.VMEM((POINTS, 128), F32)],
        [vmem()] * 9,
        10_000_000,
        3_000_000,
        8,
    )(shape, *got, right, left, sides, state)
    adj_new = adj_new.reshape(3, 1, NODES, NODES, 8, 128).transpose(0, 1, 4, 2, 3, 5)
    return adj_new, wall.transpose(1, 0, 2)


def solution(mesh):
    return jax.shard_map(
        local,
        mesh=mesh,
        in_specs=(
            P(None, "xsec", None, None, None, "span"),
            P(None, "xsec", None, None, None, "span"),
            P(),
            P("xsec"),
            P("xsec", None),
        ),
        out_specs=(P(None, "xsec", None, None, None, "span"), P("xsec", None, "span")),
        check_vma=False,
    )
```

```python
import functools

import jax
import jax.numpy as jnp
import numpy as np
from jax import lax
from jax.experimental import pallas as pl
from jax.experimental.pallas import tpu as pltpu
from jax.sharding import PartitionSpec as P

NODES = 9
NK = 512
ADV_STEP = 0.0025
DIFFUSE = 5e-05
WALL_GAIN = 0.01
SPAN_GAIN = 1.0 / 32.0
PLANE = NODES * NODES
PAD = 88
ROWS = 3 * 2 * PAD
POINTS = 3 * PLANE * 8
COLS = 3 * NODES
F32 = jnp.float32
BF16 = jnp.bfloat16
MIB = 1 << 20


def cheb_table(number):
    degree = number - 1
    points = -np.cos(np.pi * np.arange(number) / degree)
    factor = np.where((np.arange(number) == 0) | (np.arange(number) == degree), 2.0, 1.0)
    parity = (-1.0) ** np.arange(number)
    spacing = points[:, None] - points[None, :] + np.eye(number)
    matrix = factor[:, None] * parity[:, None] * parity[None, :] / (factor[None, :] * spacing)
    matrix = matrix * (1.0 - np.eye(number))
    matrix = matrix - np.eye(number) * np.sum(matrix, axis=1)[:, None]
    return matrix.astype(np.float32)


def span_tables(modes):
    indices = np.arange(modes)
    pair_index = indices // 2
    wavenum = np.where(indices == 1, modes // 2, pair_index)
    planes = np.arange(modes)
    phases = 2.0 * np.pi * (wavenum[:, None] * planes[None, :] % modes) / modes
    basis_rows = np.where((indices % 2 == 0)[:, None], np.cos(phases), np.sin(phases))
    basis_rows = np.where((indices <= 1)[:, None], np.cos(phases), basis_rows)
    norm_gain = 1.0 / np.sqrt(modes / 2.0)
    weights_k = np.where(indices <= 1, 1.0, 2.0)
    synthesis = (basis_rows * norm_gain).astype(np.float32)
    analysis = ((basis_rows * (weights_k / (modes * norm_gain))[:, None]).T).astype(np.float32)
    slopes = np.where(indices <= 1, 0.0, pair_index * SPAN_GAIN).astype(np.float32)
    kappa_sq = ((wavenum * SPAN_GAIN) ** 2).astype(np.float32)
    return synthesis, analysis, slopes, kappa_sq


def halves(table):
    high = table.astype(jnp.bfloat16)
    return high, (table.astype(np.float64) - high.astype(np.float64)).astype(jnp.bfloat16)


DERIV = cheb_table(NODES).astype(np.float64)
INNER = DERIV[:, 1:8] @ DERIV[1:8, :]
FACED = INNER + 0.5 * np.outer(DERIV[:, 0], DERIV[0]) + 0.5 * np.outer(DERIV[:, 8], DERIV[8])


def plane_tables():
    synthesis, analysis, slopes, kappa_sq = span_tables(NK)
    wave = np.zeros((NK, NK))
    wave[1::2] = slopes[0::2, None].astype(np.float64) * synthesis[0::2]
    wave[0::2] = -slopes[1::2, None].astype(np.float64) * synthesis[1::2]
    radial = np.kron(DERIV, np.eye(NODES))
    around = np.kron(np.eye(NODES), DERIV)
    both = np.zeros((2, 2, PAD, 2, PAD))
    for layer in range(2):
        both[0, layer, :PLANE, layer, :PLANE] = radial
        both[1, layer, :PLANE, layer, :PLANE] = around
    high, low = halves(both.reshape(4 * PAD, 2 * PAD))
    slope = np.concatenate([high, low], axis=1)
    kinds = [table.astype(jnp.bfloat16) for table in (synthesis, wave, analysis)]
    return kinds[0], kinds[1], slope, kinds[2]


def smem():
    return pl.BlockSpec(memory_space=pltpu.SMEM)


def vmem():
    return pl.BlockSpec(memory_space=pltpu.VMEM)


def hbm():
    return pl.BlockSpec(memory_space=pltpu.HBM)


def in_hbm(value):
    return pltpu.with_memory_space_constraint(value, pltpu.HBM)


def call(kernel, name, outs, scratch, specs, flops, nbytes, mib):
    return pl.pallas_call(
        kernel,
        out_shape=[jax.ShapeDtypeStruct(shape, kind) for shape, kind in outs],
        in_specs=specs,
        out_specs=[vmem() for _ in outs],
        scratch_shapes=scratch,
        compiler_params=pltpu.CompilerParams(vmem_limit_bytes=mib * MIB),
        cost_estimate=pl.CostEstimate(flops=flops, bytes_accessed=nbytes, transcendentals=0),
        name=name,
    )


def repack_kernel(pos_ref, width_ref, adj_hbm, fwd_hbm, height_hbm, mask_hbm, *refs):
    shared, adj_single, fwd_single = refs[0:2], refs[2:4], refs[4:6]
    wide_adj, shape_ref = refs[6:8]
    adj_ref, fwd_ref, wide_fwd, height_ref, mask_ref, sems = refs[8:14]
    singles = (adj_single, fwd_single)
    pairs = (
        (adj_hbm, adj_ref),
        (fwd_hbm, fwd_ref),
        (height_hbm, height_ref),
        (mask_hbm, mask_ref),
    )
    copies = [
        pltpu.make_async_copy(source, target, sems.at[n])
        for n, (source, target) in enumerate(pairs)
    ]
    for copy in copies:
        copy.start()
    pos = pos_ref[0]
    keep = lax.broadcasted_iota(jnp.int32, (PAD, 128), 0) < PLANE
    for which, (x_ref, wide) in enumerate(((adj_ref, wide_adj), (fwd_ref, wide_fwd))):
        copies[which].wait()
        wide[pl.ds(0, POINTS), :] = x_ref[...].astype(F32)
        for flip, out in enumerate((*shared, *singles[which])):
            group = pos ^ flip
            for comp in range(3):
                parts = []
                for layer in range(2):
                    start = comp * PLANE * 8 + 2 * group + layer
                    rows = wide[pl.ds(start, PAD, stride=8), :]
                    parts.append(jnp.where(keep, rows, 0.0))
                block = jnp.concatenate(parts, axis=0).astype(BF16)
                at = comp * 2 * PAD + (which * ROWS if flip < 2 else 0)
                out[at : at + 2 * PAD, :] = block
    for copy in copies[2:]:
        copy.wait()

    def spread(value):
        return jnp.full((8, 128), value, F32)

    layer = lax.broadcasted_iota(jnp.int32, (8, 128), 0)
    height = spread(height_ref[0])
    for index in range(1, 8):
        height = jnp.where(layer == index, height_ref[index], height)
    shape_ref[0:8, :] = 2.0 / height
    shape_ref[8:16, :] = 2.0 / spread(width_ref[0])
    shape_ref[16:24, :] = 2.0 / spread(height_ref[2 * pos])
    shape_ref[24:32, :] = 2.0 / spread(height_ref[2 * pos + 1])
    wall = WALL_GAIN * (2.0 / spread(height_ref[0]))
    for j in range(NODES):
        shape_ref[32 + 8 * j : 40 + 8 * j, :] = wall * mask_ref[0, j].astype(F32)


def repack(pos, adj, fwd, heights, widths, mask):
    return call(
        repack_kernel,
        "span_groups",
        [((2 * ROWS, 128), BF16)] * 2
        + [((ROWS, 128), BF16)] * 4
        + [((POINTS + 56, 128), F32), ((32 + 8 * NODES, 128), F32)],
        [
            pltpu.VMEM((POINTS, 128), BF16),
            pltpu.VMEM((POINTS, 128), BF16),
            pltpu.VMEM((POINTS + 56, 128), F32),
            pltpu.SMEM((8,), F32),
            pltpu.SMEM((1, NODES), jnp.int32),
            pltpu.SemaphoreType.DMA((4,)),
        ],
        [smem()] * 2 + [hbm()] * 4,
        1_000_000,
        2_000_000,
        12,
    )(pos, widths, *map(in_hbm, (adj, fwd, heights, mask)))


def gather(ref, pos):
    parts = [ref[pl.ds(pl.multiple_of(128 * (pos ^ flip), 128), 128), :] for flip in range(4)]
    return jnp.concatenate(parts, axis=0)


def transform(pos, which, shared, single, tables, planes, zplanes, grads):
    synth_ref, wave_ref, slope_ref = tables
    rows = slice(which * ROWS, (which + 1) * ROWS)
    parts = [chunk[rows, :] for chunk in shared] + [chunk[...] for chunk in single]
    modes = jnp.concatenate(parts, axis=1)
    planes[...] = jnp.dot(modes, gather(synth_ref, pos), preferred_element_type=F32)
    zplanes[...] = jnp.dot(modes, gather(wave_ref, pos), preferred_element_type=F32)
    slope = slope_ref[...]
    for comp in range(3):
        block = planes[comp * 2 * PAD : (comp + 1) * 2 * PAD, :].astype(BF16)
        stack = jnp.concatenate([block, block], axis=0)
        grads[comp] = jnp.dot(slope, stack, preferred_element_type=F32)


def adj_kernel(pos_ref, *refs):
    transform(pos_ref[0], 0, refs[0:2], refs[2:4], refs[4:7], *refs[7:10])


def force_kernel(pos_ref, shape_ref, *refs):
    tables, an_ref = refs[4:7], refs[7]
    adj_planes, adj_zplanes, adj_grads = refs[8:11]
    outs = refs[11:15]
    fwd_planes, fwd_zplanes, fwd_grads, force = refs[15:19]
    pos = pos_ref[0]
    transform(pos, 1, refs[0:2], refs[2:4], tables, fwd_planes, fwd_zplanes, fwd_grads)
    planes, zplanes = (fwd_planes, adj_planes), (fwd_zplanes, adj_zplanes)
    grads = (fwd_grads, adj_grads)

    across = shape_ref[8:16, :]
    for layer in range(2):
        along = shape_ref[16 + 8 * layer : 24 + 8 * layer, :]
        for tile in range(PAD // 8):
            row = layer * PAD + 8 * tile
            for lane in range(0, NK, 128):
                lanes = slice(lane, lane + 128)

                def plane(which, comp):
                    at = comp * 2 * PAD + row
                    return planes[which][at : at + 8, lanes]

                def zplane(which, comp):
                    at = comp * 2 * PAD + row
                    return zplanes[which][at : at + 8, lanes]

                def grad(which, direc, comp):
                    at = direc * 2 * PAD + row
                    return grads[which][comp, at : at + 8, lanes]

                fwd_r = plane(0, 0) * along
                fwd_t = plane(0, 1) * across
                fwd_z = plane(0, 2)
                adj_p = [plane(1, comp) for comp in range(3)]
                pulled = [
                    along * sum(adj_p[comp] * grad(0, 0, comp) for comp in range(3)),
                    across * sum(adj_p[comp] * grad(0, 1, comp) for comp in range(3)),
                    sum(adj_p[comp] * zplane(0, comp) for comp in range(3)),
                ]
                for comp in range(3):
                    carried = (
                        fwd_r * grad(1, 0, comp) + fwd_t * grad(1, 1, comp) + fwd_z * zplane(1, comp)
                    )
                    at = comp * 2 * PAD + row
                    force[at : at + 8, lanes] = carried - pulled[comp]

    def pick(ref):
        return jnp.concatenate([ref[pos ^ flip] for flip in range(4)], axis=1)

    analysis = pick(an_ref)
    result = jnp.dot(
        force[...].astype(BF16), analysis, preferred_element_type=F32
    ).astype(BF16)
    for flip, out in enumerate(outs):
        out[...] = result[:, 128 * flip : 128 * (flip + 1)]


def plane_shapes():
    return [(ROWS, NK), (ROWS, NK), (3, 4 * PAD, NK)]


def adj_side(pos, shared, single, tables):
    return call(
        adj_kernel,
        "adjoint_planes",
        [(shape, F32) for shape in plane_shapes()],
        [],
        [smem()] + [vmem()] * 7,
        1_500_000_000,
        8_000_000,
        12,
    )(pos, *shared, *single, *tables)


def forcing(pos, shape, shared, single, tables, adj_fields):
    return call(
        force_kernel,
        "adjoint_forcing",
        [((ROWS, 128), BF16)] * 4,
        [pltpu.VMEM(dims, F32) for dims in plane_shapes()] + [pltpu.VMEM((ROWS, NK), F32)],
        [smem()] + [vmem()] * 12,
        2_500_000_000,
        8_000_000,
        20,
    )(pos, shape, *shared, *single, *tables, *adj_fields)


def mirror(matrix):
    even = np.concatenate(
        [0.5 * (matrix[:5, :4] + matrix[:5, :4:-1]), matrix[:5, 4:5]], axis=1
    )
    odd = 0.5 * (matrix[:4, :4] - matrix[:4, :4:-1])
    return even, odd


def weighted(coeffs, values):
    total = None
    for coeff, value in zip(coeffs, values):
        term = float(coeff) * value
        total = term if total is None else total + term
    return total


def parity(values):
    even = [values[n] + values[8 - n] for n in range(4)] + [values[4]]
    odd = [values[n] - values[8 - n] for n in range(4)]
    return even, odd


def ends(even, odd):
    row_even = np.concatenate([0.5 * (DERIV[0, :4] + DERIV[0, :4:-1]), DERIV[0, 4:5]])
    row_odd = 0.5 * (DERIV[0, :4] - DERIV[0, :4:-1])
    first, second = weighted(row_even, even), weighted(row_odd, odd)
    return second + first, second - first


def unfold(even, odd):
    low = [even[n] + odd[n] for n in range(4)]
    high = [even[n] - odd[n] for n in range(4)]
    return low + [even[4]] + high[::-1]


def wave_squares(pos):
    index = lax.broadcasted_iota(jnp.int32, (8, 128), 1) + 128 * pos
    wave = jnp.where(index == 1, NK // 2, index >> 1).astype(F32) * SPAN_GAIN
    return wave * wave


def layer_vectors(shape_ref):
    layer = lax.broadcasted_iota(jnp.int32, (8, 128), 0)
    along = shape_ref[0:8, :]
    below = pltpu.roll(along, 1, 0)
    above = pltpu.roll(along, 7, 0)
    bottom, top = layer == 0, layer == 7
    own_low = jnp.where(bottom, 1.0, 0.5)
    own_high = jnp.where(top, 1.0, 0.5)
    from_below = jnp.where(bottom, 0.0, 0.5)
    from_above = jnp.where(top, 0.0, 0.5)
    return dict(
        layer=layer,
        along=along,
        across=shape_ref[8:16, :],
        own_low=own_low,
        own_high=own_high,
        from_below=from_below,
        from_above=from_above,
        grad_below=from_below * below / along,
        grad_above=from_above * above / along,
    )


def local_step(vec, kappa, load, store, sent, two_away, visc, faces):
    across = vec["across"]
    scale_t = DIFFUSE * across * across
    scale_r = DIFFUSE * vec["along"] * vec["along"]
    scale_k = DIFFUSE * kappa
    even_t, odd_t = mirror(FACED)
    even_r, odd_r = mirror(INNER)
    mix_even = 0.5 * (DERIV[:5, 0] - DERIV[:5, 8])
    mix_odd = 0.5 * (DERIV[:4, 0] + DERIV[:4, 8])

    def shared(low, high):
        low_new = vec["own_low"] * low + vec["from_below"] * pltpu.roll(high, 1, 0)
        high_new = vec["own_high"] * high + vec["from_above"] * pltpu.roll(low, 7, 0)
        return low_new, high_new

    right_ref, left_ref = sent
    right_far, left_far = two_away

    for comp in range(3):
        edge_low, edge_high = [], []
        for i in range(NODES):
            values = [load(comp, i, j) for j in range(NODES)]
            even, odd = parity(values)
            low, high = ends(even, odd)
            edge_low.append(across * low)
            edge_high.append(across * high)
            even_out = [weighted(even_t[n], even) for n in range(5)]
            odd_out = [weighted(odd_t[n], odd) for n in range(4)]
            for j, value in enumerate(unfold(even_out, odd_out)):
                visc[pl.ds(8 * (i * NODES + j), 8), :] = scale_t * value
        for edge, ref in ((edge_low, 0), (edge_high, 1)):
            edge[0], edge[8] = shared(edge[0], edge[8])
            for i in range(NODES):
                faces[pl.ds(8 * ((ref * 3 + comp) * NODES + i), 8), :] = edge[i]
        for j in range(NODES):
            values = [load(comp, i, j) for i in range(NODES)]
            even, odd = parity(values)
            low, high = ends(even, odd)
            low_mean = vec["own_low"] * low + vec["grad_below"] * pltpu.roll(high, 1, 0)
            high_mean = vec["own_high"] * high + vec["grad_above"] * pltpu.roll(low, 7, 0)
            differ, total = low_mean - high_mean, low_mean + high_mean
            even_out = [
                weighted(even_r[n], even) + float(mix_even[n]) * differ for n in range(5)
            ]
            odd_out = [weighted(odd_r[n], odd) + float(mix_odd[n]) * total for n in range(4)]
            lap = [
                scale_r * value - scale_k * values[i] + visc[pl.ds(8 * (i * NODES + j), 8), :]
                for i, value in enumerate(unfold(even_out, odd_out))
            ]
            lap[0], lap[8] = shared(lap[0], lap[8])
            if j == 0 or j == 8:
                ref, side = (left_ref, 0) if j == 0 else (right_ref, 1)
                for i in range(NODES):
                    edge = faces[pl.ds(8 * ((side * 3 + comp) * NODES + i), 8), :]
                    pair = jnp.concatenate([edge, lap[i]], axis=0).astype(BF16)
                    ref[pl.ds(16 * (comp * NODES + i), 16), :] = pair
            for i in range(NODES):
                step = 0.5 * lap[i] if j == 0 or j == 8 else lap[i]
                store(comp, i, j, values[i], step)
    for side, ref in ((0, left_far), (1, right_far)):
        for block in range(14):
            first = faces[pl.ds(8 * (side * COLS + 2 * block), 8), :]
            if 2 * block + 1 < COLS:
                second = faces[pl.ds(8 * (side * COLS + 2 * block + 1), 8), :]
            else:
                second = jnp.zeros((8, 128), F32)
            ref[pl.ds(16 * block, 16), :] = jnp.concatenate([first, second], axis=0).astype(BF16)


def spot(comp, i, j):
    return pl.ds(8 * ((comp * NODES + i) * NODES + j), 8)


def first_kernel(pos_ref, shape_ref, wide, *refs):
    given, refs = refs[0:4], refs[4:]
    out, right, left, right_far, left_far = refs[0:5]
    tables, (visc, faces, sems) = refs[5:9], refs[9:12]
    copies = [
        pltpu.make_async_copy(source, target, sems.at[n])
        for n, (source, target) in enumerate(zip(given, tables))
    ]
    for copy in copies:
        copy.start()

    def load(comp, i, j):
        return wide[spot(comp, i, j), :]

    def store(comp, i, j, value, step):
        out[spot(comp, i, j), :] = value + step

    vec = layer_vectors(shape_ref)
    kappa = wave_squares(pos_ref[0])
    local_step(vec, kappa, load, store, (right, left), (right_far, left_far), visc, faces)
    across = vec["across"]
    high = across.astype(BF16).astype(F32)
    mid = (across - high).astype(BF16).astype(F32)
    low = across - high - mid
    layer = vec["layer"]
    note = jnp.where(layer == 0, high, jnp.where(layer == 1, mid, jnp.where(layer == 2, low, 0.0)))
    block = jnp.concatenate([note, jnp.zeros((8, 128), F32)], axis=0).astype(BF16)
    for ref in (right, left):
        ref[pl.ds(16 * COLS, 16), :] = block
    for copy in copies:
        copy.wait()


def second_kernel(pos_ref, shape_ref, base_ref, *refs):
    chunks = refs[:4]
    out, right, left, right_far, left_far, push, wide, visc, faces = refs[4:]
    pos = pos_ref[0]
    for flip, chunk in enumerate(chunks):
        group = pos ^ flip
        for comp in range(3):
            block = ADV_STEP * chunk[comp * 2 * PAD : (comp + 1) * 2 * PAD, :].astype(F32)
            for layer in range(2):
                start = comp * PLANE * 8 + 2 * group + layer
                push[pl.ds(start, PLANE, stride=8), :] = block[layer * PAD : layer * PAD + PLANE]
    vec = layer_vectors(shape_ref)
    off_wall = jnp.where(vec["layer"] == 0, 0.0, 1.0)
    for comp in range(3):
        for i in range(NODES):
            for j in range(NODES):
                at = spot(comp, i, j)
                value = base_ref[at, :] + push[at, :]
                wide[at, :] = value * off_wall if i == 0 else value

    def load(comp, i, j):
        return wide[spot(comp, i, j), :]

    def store(comp, i, j, value, step):
        at = spot(comp, i, j)
        out[at, :] = value + push[at, :] + step

    local_step(
        vec,
        wave_squares(pos),
        load,
        store,
        (right, left),
        (right_far, left_far),
        visc,
        faces,
    )


def join_step(shape_ref, near, far, own, sides, state, store):
    from_left, from_right = near
    far_left, far_right = far
    own_right, own_left = own
    across = shape_ref[8:16, :]
    gain = (0.5 * DIFFUSE) * across
    gain_left, gain_right = (0.5 * DIFFUSE) * sides[0], (0.5 * DIFFUSE) * sides[1]
    for block in range(14):
        far_l = far_left[pl.ds(16 * block, 16), :].astype(F32)
        far_r = far_right[pl.ds(16 * block, 16), :].astype(F32)
        for half in range(2):
            col = 2 * block + half
            if col >= COLS:
                continue
            comp, i = divmod(col, NODES)
            at = pl.ds(16 * col, 16)
            pair_l, pair_r = from_left[at, :].astype(F32), from_right[at, :].astype(F32)
            mine_low = own_left[at, :].astype(F32)[0:8]
            mine_high = own_right[at, :].astype(F32)[0:8]
            grad_l, grad_r = gain * pair_l[0:8], gain * pair_r[0:8]
            two_l, two_r = far_l[8 * half : 8 * half + 8], far_r[8 * half : 8 * half + 8]
            for j in range(NODES):
                add = float(DERIV[j, 0]) * grad_l + float(DERIV[j, 8]) * grad_r
                if j == 0:
                    other = gain_left * (float(DERIV[8, 0]) * two_l + float(DERIV[8, 8]) * mine_low)
                    add = 0.5 * (add + pair_l[8:16] + other)
                if j == 8:
                    other = gain_right * (float(DERIV[0, 0]) * mine_high + float(DERIV[0, 8]) * two_r)
                    add = 0.5 * (add + pair_r[8:16] + other)
                store(comp, i, j, state[spot(comp, i, j), :] + add)


def first_join_kernel(shape_ref, *refs):
    near, far, own = refs[0:2], refs[2:4], refs[4:6]
    state, out, sides_out = refs[6:9]
    sides = []
    for side, ref in enumerate(near):
        note = ref[pl.ds(16 * COLS, 16), :].astype(F32)[0:8]
        value = jnp.broadcast_to(jnp.sum(note, axis=0, keepdims=True), (8, 128))
        sides_out[pl.ds(8 * side, 8), :] = value
        sides.append(value)

    def store(comp, i, j, value):
        out[spot(comp, i, j), :] = value

    join_step(shape_ref, near, far, own, sides, state, store)


def second_join_kernel(shape_ref, *refs):
    near, far, own = refs[0:2], refs[2:4], refs[4:6]
    sides_ref, state, out, wall, full = refs[6:11]
    sides = [sides_ref[pl.ds(0, 8), :], sides_ref[pl.ds(8, 8), :]]
    layer = lax.broadcasted_iota(jnp.int32, (8, 128), 0)
    off_wall = jnp.where(layer == 0, 0.0, 1.0)

    def store(comp, i, j, value):
        full[spot(comp, i, j), :] = value * off_wall if i == 0 else value

    join_step(shape_ref, near, far, own, sides, state, store)
    out[...] = full[...].astype(BF16)
    for j in range(NODES):
        rows = weighted(DERIV[0], [full[spot(0, i, j), :] for i in range(NODES)])
        rows = rows * shape_ref[pl.ds(32 + 8 * j, 8), :]
        wall[j] = rows[0:1]


def ring(value, shift):
    count = lax.axis_size("xsec")
    return lax.ppermute(value, "xsec", [(n, (n + shift) % count) for n in range(count)])


def swap(value, flip):
    return lax.ppermute(value, "span", [(n, n ^ flip) for n in range(lax.axis_size("span"))])


def halo(right, left, shift):
    return [ring(right, shift), ring(left, -shift)]


def local(fwd_modes, adj_modes, layer_height, column_width, wall_mask):
    synth, wave, slope, analysis = plane_tables()
    analysis = analysis.reshape(NK, 4, 128).transpose(1, 0, 2)
    constants = [jnp.asarray(table) for table in (synth, wave, slope, analysis)]
    pos = lax.axis_index("span").astype(jnp.int32).reshape(1)

    def resident(field):
        return field.transpose(0, 1, 3, 4, 2, 5).reshape(POINTS, 128)

    fwd_flat, adj_flat = resident(fwd_modes), resident(adj_modes)
    state_shape = ((POINTS, 128), F32)
    far_shapes = [((224, 128), BF16)] * 2
    work = [pltpu.VMEM((PLANE * 8, 128), F32), pltpu.VMEM((2 * COLS * 8, 128), F32)]

    def exchange(parts):
        return [parts[0]] + [swap(part, flip + 1) for flip, part in enumerate(parts[1:])]

    own, sibling, adj_2, adj_3, fwd_2, fwd_3, adj_wide, shape = repack(
        pos, adj_flat, fwd_flat, layer_height, column_width, wall_mask
    )
    shared = [own, swap(sibling, 1)]
    adj_away, fwd_away = [swap(adj_2, 2), swap(adj_3, 3)], [swap(fwd_2, 2), swap(fwd_3, 3)]

    state, right, left, right_far, left_far, *tables = call(
        first_kernel,
        "first_substep",
        [state_shape]
        + [((16 * COLS + 16, 128), BF16)] * 2
        + far_shapes
        + [(table.shape, BF16) for table in constants],
        work + [pltpu.SemaphoreType.DMA((4,))],
        [smem()] + [vmem()] * 2 + [hbm()] * 4,
        50_000_000,
        3_000_000,
        10,
    )(pos, shape, adj_wide, *map(in_hbm, constants))
    near_right, near_left, *adj_away = lax.optimization_barrier((right, left, *adj_away))
    near = halo(near_right, near_left, 1)
    adj_fields = adj_side(pos, shared, adj_away, tables[:3])
    parts = forcing(pos, shape, shared, fwd_away, tables, adj_fields)
    parts = list(parts)
    right_far, left_far, *near, parts[0] = lax.optimization_barrier(
        (right_far, left_far, *near, parts[0])
    )
    parts = exchange(parts)
    far = halo(right_far, left_far, 2)

    base, sides = call(
        first_join_kernel,
        "first_join",
        [state_shape, ((16, 128), F32)],
        [],
        [vmem()] * 8,
        10_000_000,
        3_000_000,
        8,
    )(shape, *near, *far, right, left, state)

    state, right, left, right_far, left_far = call(
        second_kernel,
        "second_substep",
        [state_shape] + [((16 * COLS, 128), BF16)] * 2 + far_shapes,
        [pltpu.VMEM((POINTS, 128), F32)] * 2 + work,
        [smem()] + [vmem()] * 6,
        50_000_000,
        4_000_000,
        12,
    )(pos, shape, base, *parts)
    got = halo(right, left, 1) + halo(right_far, left_far, 2)

    adj_new, wall = call(
        second_join_kernel,
        "second_join",
        [((POINTS, 128), BF16), ((NODES, 1, 128), F32)],
        [pltpu.VMEM((POINTS, 128), F32)],
        [vmem()] * 9,
        10_000_000,
        3_000_000,
        8,
    )(shape, *got, right, left, sides, state)
    adj_new = adj_new.reshape(3, 1, NODES, NODES, 8, 128).transpose(0, 1, 4, 2, 3, 5)
    return adj_new, wall.transpose(1, 0, 2)


def solution(mesh):
    return jax.shard_map(
        local,
        mesh=mesh,
        in_specs=(
            P(None, "xsec", None, None, None, "span"),
            P(None, "xsec", None, None, None, "span"),
            P(),
            P("xsec"),
            P("xsec", None),
        ),
        out_specs=(P(None, "xsec", None, None, None, "span"), P("xsec", None, "span")),
        check_vma=False,
    )
```
